512 devices in a mesh: img: 16 (over z), tile: 32 (over x, y, core).
Axes of the slice: x: 4, y: 4, z: 16, core: 2. Of those that a mesh axis runs over, the one named last changes fastest.
Arguments:
- features: bfloat16 [16, 512, 64, 256], P('img', 'tile'), may hold values from -6 to 6
- weight: bfloat16 [3, 3, 256, 256], replicated, may hold values from -0.125 to 0.125
- pool_grad: bfloat16 [16, 512, 7, 7, 256], P('img', 'tile'), may hold values from -6 to 6
- hard_index: int32 [16, 512], P('img', 'tile'), may hold values from 0 to 19999, as said below
- boxes: int32 [16, 20000, 4], P('img'), may hold values from 0 to 498, as said below
Outputs:
- x_grad: bfloat16 [16, 512, 64, 256], P('img', 'tile')
- weight_grad: float32 [256, 3, 3, 256], P('tile')
The draws below stay inside these ranges and needn't reach their ends.
Inputs may be any that keep to these rules, and one draw needn't show every extreme that they name: `hard_index`: among the 16 entries of one tile index's block, at most 2 choose boxes whose top row lies in any one tile (rows t * 16 to t * 16 + 15); in every image some tile receives exactly 2 from every block.
All inputs are finite; a program needn't handle non-finite values.
Results may differ from the reference program's by a relative error of at most 0.0058.
Values may be sent and summed in bfloat16 or wider, within the bound.
No kernel may reach another device: no remote copies, remote signals or barrier semaphores. Data moves between devices by JAX's collectives and lax.ppermute only.
A program may use at most 64 MiB of HBM per device.

```python
import jax
import jax.numpy as jnp
from jax import lax

C = 256
TR = 16
MW = 64
ROI_DEV = 16
CAP = 2
REACH = 14
BINS = 7
PROPS = 20000
IMAGES = 16
H = 512
ROIS = 512
N_TILE = 32


def box_table(key):

    def one_image(image_key):
        keys = jax.random.split(image_key, 6)
        owners = jax.random.randint(keys[0], (PROPS,), 0, N_TILE)
        cover = jax.random.permutation(keys[1], PROPS)[:N_TILE]
        owners = owners.at[cover].set(jnp.arange(N_TILE, dtype=jnp.int32))
        top_row = jnp.minimum(owners * TR + jax.random.randint(keys[2], (PROPS,), 0, TR), TR * N_TILE - REACH)
        row_step = jax.random.randint(keys[3], (PROPS,), 1, 3)
        col_step = jax.random.randint(keys[4], (PROPS,), 1, 4)
        left_col = jax.random.randint(keys[5], (PROPS,), 0, MW - 1 - 6 * col_step)
        return jnp.stack([top_row, left_col, row_step, col_step], axis=1).astype(jnp.int32)
    return jax.vmap(one_image)(jax.random.split(key, IMAGES))


def draw_boxes(key, part):
    return box_table(key)


def draw_hard_index(key, part):
    table = box_table(key)
    key = jax.random.fold_in(key, 7)

    def one_image(image_key, image_table):
        owners = image_table[:, 0] // TR
        order = jnp.argsort(owners, stable=True).astype(jnp.int32)
        counts = jnp.sum((owners[None, :] == jnp.arange(N_TILE, dtype=jnp.int32)[:, None]).astype(jnp.int32), axis=1)
        starts = jnp.cumsum(counts) - counts
        keys = jax.random.split(image_key, 3)
        hottest = jax.random.randint(keys[0], (), 0, N_TILE)
        choices_pool = jnp.arange(2 * (N_TILE - 1), dtype=jnp.int32) // 2
        offsets = jax.vmap(lambda small_key: jax.random.permutation(small_key, choices_pool)[:ROI_DEV - CAP])(jax.random.split(keys[1], N_TILE))
        rest = (hottest + 1 + offsets) % N_TILE
        target = jnp.concatenate([jnp.full((N_TILE, CAP), hottest, jnp.int32), rest.astype(jnp.int32)], axis=1).reshape(ROIS)
        within = jax.random.randint(keys[2], (ROIS,), 0, counts[target])
        return order[starts[target] + within].astype(jnp.int32)
    return jax.vmap(one_image)(jax.random.split(key, IMAGES), table)


def block_scale(stream_key, extent, cuts, least, largest):
    def one(dim, parts):
        heights = jax.random.uniform(jax.random.fold_in(jax.random.fold_in(stream_key, 6), dim), (parts,), jnp.float32, least / len(cuts), largest / len(cuts))
        return jnp.repeat(jnp.exp(heights), extent[dim] // parts).reshape((-1,) + (1,) * (len(extent) - dim - 1))

    gain = one(*cuts[0])
    for cut in cuts[1:]:
        gain = gain * one(*cut)
    return gain


def normal_values(own_key, dims, width, most, cuts=(), kind=jnp.bfloat16):
    drawn = width * jax.random.normal(own_key, dims, jnp.float32)
    if cuts:
        drawn = drawn * block_scale(own_key, dims, cuts, -0.22, 0.18)
    return jnp.clip(drawn, -most, most).astype(kind)


def setup_inputs(seed: int = 0) -> dict:
    streams_of = jax.random.split(jax.random.key(seed), 6)
    return {
        "features": normal_values(streams_of[0], (IMAGES, H, MW, C), 1.0, 6.0, ((0, 16), (1, 32))),
        "weight": normal_values(streams_of[1], (3, 3, C, C), (9 * C) ** -0.5, 0.125),
        "pool_grad": normal_values(streams_of[2], (IMAGES, ROIS, BINS, BINS, C), 1.0, 6.0, ((0, 16), (1, 32))),
        "hard_index": draw_hard_index(jax.random.fold_in(streams_of[5], 71), 0),
        "boxes": draw_boxes(jax.random.fold_in(streams_of[5], 71), 0),
    }


FRAC_ROW = 0.25
FRAC_COL = 0.75


def bin_weights(start, step, length, frac):
    places = start[:, None] + jnp.arange(BINS, dtype=jnp.int32)[None, :] * step[:, None]
    grid = jnp.arange(length, dtype=jnp.int32)[None, None, :]
    near = jnp.where(grid == places[:, :, None], 1.0 - frac, 0.0)
    beyond = jnp.where(grid == places[:, :, None] + 1, frac, 0.0)
    return (near + beyond).astype(jnp.float32)


def reference(features, weight, pool_grad, hard_index, boxes):
    block_size = 16

    def one_image(items):
        inputs, grads, picks, table = items
        chosen = table[picks]
        row_weight = bin_weights(chosen[:, 0], chosen[:, 2], H, FRAC_ROW)
        col_weight = bin_weights(chosen[:, 1], chosen[:, 3], MW, FRAC_COL)
        count = ROIS // block_size

        def add_block(running, pieces):
            grad_block, row_block, col_block = pieces
            spread = jnp.einsum("sijc,sjw->siwc", grad_block.astype(jnp.float32), col_block).astype(jnp.bfloat16)
            rows_left = row_block.reshape(block_size * BINS, H).astype(jnp.bfloat16)
            update = jnp.dot(rows_left.T, spread.reshape(block_size * BINS, MW * C), preferred_element_type=jnp.float32)
            return running + update, None

        summed, unused_out = lax.scan(
            add_block,
            jnp.zeros((H, MW * C), jnp.float32),
            (grads.reshape(count, block_size, BINS, BINS, C),
             row_weight.reshape(count, block_size, BINS, H),
             col_weight.reshape(count, block_size, BINS, MW)))
        map_grad = summed.reshape(H, MW, C).astype(jnp.bfloat16)
        padded = jnp.pad(map_grad, ((1, 1), (1, 1), (0, 0)))
        flat_in = inputs.reshape(H * MW, C)
        input_grad = jnp.zeros((H * MW, C), jnp.float32)
        filter_parts = []
        for row_off in range(3):
            for col_off in range(3):
                window = padded[2 - row_off:2 - row_off + H, 2 - col_off:2 - col_off + MW].reshape(H * MW, C)
                input_grad = input_grad + jnp.dot(window, weight[row_off, col_off].T, preferred_element_type=jnp.float32)
                filter_parts.append(jnp.dot(flat_in.T, window, preferred_element_type=jnp.float32))
        filter_grad = jnp.stack(filter_parts, axis=1).reshape(C, 3, 3, C)
        return input_grad.reshape(H, MW, C).astype(jnp.bfloat16), filter_grad

    x_grad, filter_all = lax.map(one_image, (features, pool_grad, hard_index, boxes))
    return x_grad, jnp.sum(filter_all, axis=0) / IMAGES
```

```python
import jax
import jax.numpy as jnp
from jax import lax
from jax.experimental import pallas as pl
from jax.experimental.pallas import tpu as pltpu
from jax.sharding import Mesh, PartitionSpec as P

C = 256
TR = 16
MW = 64
ROI_DEV = 16
CAP = 2
REACH = 14
BINS = 7
CELLS = BINS * BINS
PROPS = 20000
TILES = 32
IMAGES = 16
EXT = TR + REACH - 1
SLOT = CELLS + 1
BLOCK = 104
SLOTS = TILES * CAP
KDIM = TILES * BLOCK
LANES = 128
WHOLE = PROPS // LANES * LANES
F32 = jnp.float32
BF16 = jnp.bfloat16
I32 = jnp.int32
VMEM_BYTES = 56 * 1024 * 1024
CIN = C // TILES
NPART = 9 * CIN


def vmem():
    return pl.BlockSpec(memory_space=pltpu.VMEM)


def iota(shape, dim):
    return lax.broadcasted_iota(I32, shape, dim)


def dispatch_kernel(index_ref, boxes_ref, grad_ref, out_ref):
    lane16 = iota((4, ROI_DEV), 1)
    lanes = iota((4, LANES), 1)
    tail = jnp.concatenate(
        [boxes_ref[:, WHOLE:], jnp.zeros((4, LANES - (PROPS - WHOLE)), I32)], axis=1
    )
    chosen = jnp.zeros((4, ROI_DEV), I32)
    for r in range(ROI_DEV):
        index = index_ref[0, r]
        block = index // LANES
        at = jnp.minimum(block, WHOLE // LANES - 1) * LANES
        row = jnp.where(
            block == WHOLE // LANES, tail, boxes_ref[:, pl.ds(pl.multiple_of(at, LANES), LANES)]
        )
        found = jnp.sum(jnp.where(lanes == index - block * LANES, row, 0), axis=1, keepdims=True)
        chosen = jnp.where(lane16 == r, found, chosen)
    chosen = chosen.astype(F32)
    top = chosen[0:1]
    owner = jnp.floor(top * (1.0 / TR))
    local_top = top - owner * TR
    diag = iota((ROI_DEV, ROI_DEV), 0) == iota((ROI_DEV, ROI_DEV), 1)

    def column(row):
        wide = jnp.broadcast_to(row, (ROI_DEV, ROI_DEV))
        return jnp.sum(jnp.where(diag, wide, 0.0), axis=1, keepdims=True)

    before = iota((ROI_DEV, ROI_DEV), 0) < iota((ROI_DEV, ROI_DEV), 1)
    same = column(owner) == owner
    rank = jnp.sum(jnp.where(before & same, 1.0, 0.0), axis=0, keepdims=True)
    field = iota((ROI_DEV, C), 1)
    box_rows = jnp.zeros((ROI_DEV, C), F32)
    for f, row in enumerate((local_top, chosen[1:2], chosen[2:3], chosen[3:4])):
        box_rows = jnp.where(field == f, column(row), box_rows)
    depth = SLOT * ROI_DEV
    wide = jnp.concatenate([owner, rank, jnp.zeros((6, ROI_DEV), F32)], axis=0).astype(BF16)
    spreading = iota((ROI_DEV, depth), 1) % ROI_DEV == iota((ROI_DEV, depth), 0)
    spread = jnp.dot(wide, spreading.astype(F32).astype(BF16), preferred_element_type=F32)
    cell = (iota((1, depth), 1) // ROI_DEV).astype(F32)
    goal = (spread[0:1] * BLOCK + spread[1:2] * SLOT + cell).astype(I32)
    source = jnp.concatenate(
        [grad_ref[...].reshape(CELLS * ROI_DEV, C), box_rows.astype(BF16)], axis=0
    )
    step = KDIM // 8
    for m in range(8):
        place = iota((step, depth), 0) + m * step == goal
        out_ref[m * 4 : m * 4 + 4] = (
            jnp.dot(place.astype(F32).astype(BF16), source, preferred_element_type=F32)
            .astype(BF16)
            .reshape(4, BLOCK, C)
        )


def dispatch(index, boxes_t, grads):
    return pl.pallas_call(
        dispatch_kernel,
        out_shape=jax.ShapeDtypeStruct((TILES, BLOCK, C), BF16),
        in_specs=[pl.BlockSpec(memory_space=pltpu.SMEM), vmem(), vmem()],
        out_specs=vmem(),
        compiler_params=pltpu.CompilerParams(vmem_limit_bytes=VMEM_BYTES),
        name="dispatch",
    )(index, boxes_t, grads)


def weights_of(got_ref, rows_ref, cols_ref):
    slot = iota((SLOTS, KDIM), 0)
    cell = iota((SLOTS, KDIM), 1)
    first = (slot // CAP) * BLOCK + (slot % CAP) * SLOT
    pick = (cell == first + CELLS).astype(F32).astype(BF16)
    box = jnp.dot(pick, got_ref[...].reshape(KDIM, C), preferred_element_type=F32)
    box = box[:, :LANES].T[:8].astype(BF16)
    cover = ((cell >= first) & (cell < first + CELLS)).astype(F32).astype(BF16)
    field = jnp.dot(box, cover, preferred_element_type=F32).astype(I32)
    within = iota((1, KDIM), 1) % BLOCK
    inside = within < CAP * SLOT
    within = within % SLOT
    inside = inside & (within < CELLS)
    row_bin = within // BINS
    col_bin = within - row_bin * BINS
    row = jnp.where(inside, field[0:1] + row_bin * field[2:3], -9)
    col = field[1:2] + col_bin * field[3:4]
    grid = iota((32, KDIM), 0)
    rows_ref[...] = jnp.where(grid == row, 0.75, jnp.where(grid == row + 1, 0.25, 0.0))
    grid = iota((MW, KDIM), 0)
    cols_ref[...] = jnp.where(grid == col, 0.25, jnp.where(grid == col + 1, 0.75, 0.0)).astype(BF16)


def rows_of(start, count, got_ref, rows_ref, cols_ref, left_ref):
    cols = cols_ref[...]
    for h in range(count):
        left_ref[h * MW : (h + 1) * MW] = cols * rows_ref[start + h : start + h + 1, :].astype(BF16)
    return jnp.dot(
        left_ref[: count * MW], got_ref[...].reshape(KDIM, C), preferred_element_type=F32
    )


def scatter_kernel(got_ref, own_ref, above_ref, below_ref, rows_ref, cols_ref, left_ref):
    weights_of(got_ref, rows_ref, cols_ref)
    for start, count in ((0, 8), (8, 8), (16, 8), (24, 5)):
        part = rows_of(start, count, got_ref, rows_ref, cols_ref, left_ref)
        if start < TR:
            own_ref[start * MW : (start + count) * MW] = part
        if start == 0:
            below_ref[...] = part[:MW].astype(BF16)
        if start == 8:
            above_ref[:MW] = part[7 * MW :].astype(BF16)
        if start == 16:
            own_ref[TR * MW :] = part[:MW]
            above_ref[MW : 9 * MW] = part.astype(BF16)
        if start == 24:
            above_ref[9 * MW :] = part.astype(BF16)


def scatter(got):
    return pl.pallas_call(
        scatter_kernel,
        out_shape=(
            jax.ShapeDtypeStruct(((TR + 1) * MW, C), F32),
            jax.ShapeDtypeStruct((REACH * MW, C), BF16),
            jax.ShapeDtypeStruct((MW, C), BF16),
        ),
        in_specs=[vmem()],
        out_specs=(vmem(), vmem(), vmem()),
        scratch_shapes=[
            pltpu.VMEM((32, KDIM), F32),
            pltpu.VMEM((MW, KDIM), BF16),
            pltpu.VMEM((8 * MW, KDIM), BF16),
        ],
        compiler_params=pltpu.CompilerParams(vmem_limit_bytes=VMEM_BYTES),
        name="scatter",
    )(got)


def filter_kernel(own_ref, above_ref, below_ref, features_ref, part_ref, shifted_ref):
    rows = (TR + 2) * MW
    whole = jnp.concatenate(
        [
            above_ref[:MW].astype(F32),
            own_ref[: (REACH - 1) * MW] + above_ref[MW:].astype(F32),
            own_ref[(REACH - 1) * MW : TR * MW],
            own_ref[TR * MW :] + below_ref[...].astype(F32),
        ],
        axis=0,
    )
    column = iota((rows, C), 0) % MW
    shifted_ref[0] = jnp.where(column == MW - 1, 0.0, pltpu.roll(whole, rows - 1, 0)).astype(BF16)
    shifted_ref[1] = whole.astype(BF16)
    shifted_ref[2] = jnp.where(column == 0, 0.0, pltpu.roll(whole, 1, 0)).astype(BF16)
    turned = features_ref[...].T
    for a in range(3):
        for e in range(3):
            part = jnp.dot(
                turned,
                shifted_ref[e, (2 - a) * MW : (2 - a + TR) * MW],
                preferred_element_type=F32,
            )
            at = (a * 3 + e) * CIN
            part_ref[:, at : at + CIN, :] = part.reshape(TILES, CIN, C).astype(BF16)


def filter_part(own, above, below, features):
    return pl.pallas_call(
        filter_kernel,
        out_shape=(
            jax.ShapeDtypeStruct((TILES, NPART, C), BF16),
            jax.ShapeDtypeStruct((3, (TR + 2) * MW, C), BF16),
        ),
        in_specs=[vmem()] * 4,
        out_specs=(vmem(), vmem()),
        compiler_params=pltpu.CompilerParams(vmem_limit_bytes=VMEM_BYTES),
        name="filter",
    )(own, above, below, features)


def input_kernel(shifted_ref, weight_ref, out_ref):
    total = jnp.zeros((TR * MW, C), F32)
    for a in range(3):
        for e in range(3):
            total = total + lax.dot_general(
                shifted_ref[e, (2 - a) * MW : (2 - a + TR) * MW],
                weight_ref[a * 3 + e],
                (((1,), (1,)), ((), ())),
                preferred_element_type=F32,
            )
    out_ref[...] = total.astype(BF16)


def input_part(shifted, weight):
    return pl.pallas_call(
        input_kernel,
        out_shape=jax.ShapeDtypeStruct((TR * MW, C), BF16),
        in_specs=[vmem()] * 2,
        out_specs=vmem(),
        compiler_params=pltpu.CompilerParams(vmem_limit_bytes=VMEM_BYTES),
        name="input",
        cost_estimate=pl.CostEstimate(
            flops=2 * TR * MW * 9 * C * C, bytes_accessed=4 << 20, transcendentals=0
        ),
    )(shifted, weight)


def body(features, weight, pool_grad, hard_index, boxes):
    grads = pool_grad[0].transpose(1, 2, 0, 3).reshape(CELLS, ROI_DEV, C)
    send = dispatch(hard_index, boxes[0].T, grads)
    got = lax.all_to_all(send, "tile", split_axis=0, concat_axis=0, tiled=True)
    own, above, below = scatter(got)
    up = [(t, t + 1) for t in range(TILES - 1)]
    above = lax.ppermute(above, "tile", up)
    below = lax.ppermute(below, "tile", [(b, a) for a, b in up])
    part, shifted = filter_part(own, above, below, features[0].reshape(TR * MW, C))
    parts = part.reshape(TILES, 4, NPART // 4, C).transpose(1, 0, 2, 3)
    parts = parts.reshape(4 * TILES, NPART // 4, C)
    parts = lax.all_to_all(parts, ("zl", "tile"), split_axis=0, concat_axis=0, tiled=True)
    x_grad = input_part(shifted, weight.reshape(9, C, C)).reshape(1, TR, MW, C)
    summed = jnp.sum(parts.astype(F32), axis=0).astype(BF16)
    copies = jnp.broadcast_to(summed[None], (IMAGES, NPART // 4, C))
    copies = lax.all_to_all(copies, ("zh", "zl"), split_axis=0, concat_axis=0, tiled=True)
    total = jnp.sum(copies.reshape(4, 4, NPART // 4, C).astype(F32), axis=0) * (1.0 / IMAGES)
    total = total.reshape(9, CIN, C).transpose(1, 0, 2).reshape(CIN, 3, 3, C)
    return x_grad, total


def solution(mesh):
    split = Mesh(mesh.devices.reshape(4, 4, TILES), ("zh", "zl", "tile"))
    images = ("zh", "zl")
    return jax.shard_map(
        body,
        mesh=split,
        in_specs=(
            P(images, "tile", None, None),
            P(),
            P(images, "tile", None, None, None),
            P(images, "tile"),
            P(images, None, None),
        ),
        out_specs=(P(images, "tile", None, None), P("tile", None, None, None)),
        check_vma=False,
    )
```

```python
import functools

import jax
import jax.numpy as jnp
from jax import lax
from jax.experimental import pallas as pl
from jax.experimental.pallas import tpu as pltpu
from jax.sharding import Mesh, PartitionSpec as P

C = 256
TR = 16
MW = 64
ROI_DEV = 16
CAP = 2
REACH = 14
BINS = 7
CELLS = BINS * BINS
PROPS = 20000
TILES = 32
IMAGES = 16
EXT = TR + REACH - 1
REACHED = 32 * MW
SLOT = CELLS + 1
BLOCK = 104
SLOTS = TILES * CAP
KDIM = TILES * BLOCK
LANES = 128
WHOLE = PROPS // LANES * LANES
F32 = jnp.float32
BF16 = jnp.bfloat16
I32 = jnp.int32
CIN = C // TILES
NPART = 9 * CIN


def vmem():
    return pl.BlockSpec(memory_space=pltpu.VMEM)


def cost(flops, moved):
    return pl.CostEstimate(flops=flops, bytes_accessed=moved, transcendentals=0)


def iota(shape, dim):
    return lax.broadcasted_iota(I32, shape, dim)


def dispatch_kernel(
    index_hbm, boxes_hbm, grad_hbm, out_hbm, index_ref, boxes_ref, source_ref, sent_ref, sems
):
    copies = [
        pltpu.make_async_copy(index_hbm, index_ref, sems.at[0]),
        pltpu.make_async_copy(boxes_hbm, boxes_ref, sems.at[1]),
        pltpu.make_async_copy(grad_hbm, source_ref.at[:CELLS], sems.at[2]),
    ]
    for copy in copies:
        copy.start()
    copies[0].wait()
    copies[1].wait()
    lane16 = iota((4, ROI_DEV), 1)
    lanes = iota((4, LANES), 1)
    tail = jnp.concatenate(
        [boxes_ref[:, WHOLE:], jnp.zeros((4, LANES - (PROPS - WHOLE)), I32)], axis=1
    )
    chosen = jnp.zeros((4, ROI_DEV), I32)
    for r in range(ROI_DEV):
        index = index_ref[0, r]
        block = index // LANES
        at = jnp.minimum(block, WHOLE // LANES - 1) * LANES
        row = jnp.where(
            block == WHOLE // LANES, tail, boxes_ref[:, pl.ds(pl.multiple_of(at, LANES), LANES)]
        )
        found = jnp.sum(jnp.where(lanes == index - block * LANES, row, 0), axis=1, keepdims=True)
        chosen = jnp.where(lane16 == r, found, chosen)
    chosen = chosen.astype(F32)
    top = chosen[0:1]
    owner = jnp.floor(top * (1.0 / TR))
    local_top = top - owner * TR
    diag = iota((ROI_DEV, ROI_DEV), 0) == iota((ROI_DEV, ROI_DEV), 1)

    def column(row):
        wide = jnp.broadcast_to(row, (ROI_DEV, ROI_DEV))
        return jnp.sum(jnp.where(diag, wide, 0.0), axis=1, keepdims=True)

    before = iota((ROI_DEV, ROI_DEV), 0) < iota((ROI_DEV, ROI_DEV), 1)
    same = column(owner) == owner
    rank = jnp.sum(jnp.where(before & same, 1.0, 0.0), axis=0, keepdims=True)
    field = iota((ROI_DEV, C), 1)
    box_rows = jnp.zeros((ROI_DEV, C), F32)
    for f, row in enumerate((local_top, chosen[1:2], chosen[2:3], chosen[3:4])):
        box_rows = jnp.where(field == f, column(row), box_rows)
    source_ref[CELLS] = box_rows.astype(BF16)
    depth = SLOT * ROI_DEV
    wide = jnp.concatenate([owner, rank, jnp.zeros((6, ROI_DEV), F32)], axis=0).astype(BF16)
    spreading = iota((ROI_DEV, depth), 1) % ROI_DEV == iota((ROI_DEV, depth), 0)
    spread = jnp.dot(wide, spreading.astype(F32).astype(BF16), preferred_element_type=F32)
    cell = (iota((1, depth), 1) // ROI_DEV).astype(F32)
    goal = (spread[0:1] * BLOCK + spread[1:2] * SLOT + cell).astype(I32)
    copies[2].wait()
    source = source_ref[...].reshape(depth, C)
    step = KDIM // 8
    sent = []
    for m in range(8):
        part = pl.ds(m * (TILES // 8), TILES // 8)
        place = iota((step, depth), 0) == goal - m * step
        sent_ref[part] = (
            jnp.dot(place.astype(F32).astype(BF16), source, preferred_element_type=F32)
            .astype(BF16)
            .reshape(TILES // 8, BLOCK, C)
        )
        sent.append(pltpu.make_async_copy(sent_ref.at[part], out_hbm.at[part], sems.at[3 + m]))
        sent[-1].start()
    for copy in sent:
        copy.wait()


def dispatch(index, boxes_t, grads):
    return pl.pallas_call(
        dispatch_kernel,
        out_shape=jax.ShapeDtypeStruct((TILES, BLOCK, C), BF16),
        in_specs=[pl.BlockSpec(memory_space=pl.ANY)] * 3,
        out_specs=pl.BlockSpec(memory_space=pl.ANY),
        scratch_shapes=[
            pltpu.SMEM((1, ROI_DEV), I32),
            pltpu.VMEM((4, PROPS), I32),
            pltpu.VMEM((SLOT, ROI_DEV, C), BF16),
            pltpu.VMEM((TILES, BLOCK, C), BF16),
            pltpu.SemaphoreType.DMA((11,)),
        ],
        compiler_params=pltpu.CompilerParams(vmem_limit_bytes=60 << 20),
        name="dispatch",
        cost_estimate=cost(2 * KDIM * SLOT * ROI_DEV * C, 3 << 20),
    )(index, boxes_t, grads)


def weights_of(got_ref, rows_ref, cols_ref):
    slot = iota((SLOTS, KDIM), 0)
    cell = iota((SLOTS, KDIM), 1)
    first = (slot % TILES) * BLOCK + (slot // TILES) * SLOT
    box = jnp.concatenate(
        [got_ref[:, s * SLOT + CELLS, :LANES].astype(F32) for s in range(CAP)], axis=0
    )
    box = box.T[:8].astype(BF16)
    cover = ((cell >= first) & (cell < first + CELLS)).astype(F32).astype(BF16)
    field = jnp.dot(box, cover, preferred_element_type=F32).astype(I32)
    within = iota((1, KDIM), 1) % BLOCK
    inside = within < CAP * SLOT
    within = within % SLOT
    inside = inside & (within < CELLS)
    row_bin = within // BINS
    col_bin = within - row_bin * BINS
    row = jnp.where(inside, field[0:1] + row_bin * field[2:3], -9)
    col = field[1:2] + col_bin * field[3:4]
    grid = iota((32, KDIM), 0)
    rows_ref[...] = jnp.where(grid == row, 0.75, jnp.where(grid == row + 1, 0.25, 0.0))
    grid = iota((MW, KDIM), 0)
    cols_ref[...] = jnp.where(grid == col, 0.25, jnp.where(grid == col + 1, 0.75, 0.0)).astype(BF16)


def rows_of(start, count, got_ref, rows_ref, cols_ref, left_ref):
    cols = cols_ref[...]
    for h in range(count):
        left_ref[h * MW : (h + 1) * MW] = cols * rows_ref[start + h : start + h + 1, :].astype(BF16)
    return jnp.dot(
        left_ref[: count * MW], got_ref[...].reshape(KDIM, C), preferred_element_type=F32
    )


def turn_kernel(before_ref, own_ref, after_ref, out_ref):
    rows = jnp.concatenate(
        [before_ref[...], own_ref[...], after_ref[...], jnp.zeros((MW, C), BF16)], axis=0
    )
    out_ref[...] = rows.T


def turn(before, own, after):
    return pl.pallas_call(
        turn_kernel,
        out_shape=jax.ShapeDtypeStruct((C, REACHED), BF16),
        in_specs=[vmem()] * 3,
        out_specs=vmem(),
        compiler_params=pltpu.CompilerParams(vmem_limit_bytes=8 << 20),
        name="turn",
        cost_estimate=cost(TR * MW * C, 2 << 20),
    )(before, own, after)


def shifts(rows):
    count = rows.shape[0]
    column = iota((count, C), 0) % MW
    return (
        jnp.where(column == MW - 1, 0.0, pltpu.roll(rows, count - 1, 0)).astype(BF16),
        rows.astype(BF16),
        jnp.where(column == 0, 0.0, pltpu.roll(rows, 1, 0)).astype(BF16),
    )


def filter_kernel(
    got_ref, turned_ref, part_ref, own_ref, above_ref, below_ref,
    rows_ref, cols_ref, left_ref, shifted_ref,
):
    weights_of(got_ref, rows_ref, cols_ref)
    shifted_ref[:, : 2 * MW] = jnp.zeros((3, 2 * MW, C), BF16)
    shifted_ref[:, (2 + EXT) * MW :] = jnp.zeros((3, 3 * MW, C), BF16)
    for start, count in ((0, 8), (8, 8), (16, 8), (24, 5)):
        part = rows_of(start, count, got_ref, rows_ref, cols_ref, left_ref)
        for e, moved in enumerate(shifts(part)):
            shifted_ref[e, (2 + start) * MW : (2 + start + count) * MW] = moved
        if start < TR:
            own_ref[start * MW : (start + count) * MW] = part
        if start == 0:
            below_ref[...] = part[:MW].astype(BF16)
        if start == 8:
            above_ref[:MW] = part[7 * MW :].astype(BF16)
        if start == 16:
            own_ref[TR * MW :] = part[:MW]
            above_ref[MW : 9 * MW] = part.astype(BF16)
        if start == 24:
            above_ref[9 * MW :] = part.astype(BF16)
    for a in range(3):
        for e in range(3):
            part = jnp.dot(
                turned_ref[...],
                shifted_ref[e, (2 - a) * MW : (2 - a) * MW + REACHED],
                preferred_element_type=F32,
            )
            at = (a * 3 + e) * CIN
            part_ref[:, at : at + CIN, :] = part.reshape(TILES, CIN, C).astype(BF16)


def filter_part(got, turned):
    return pl.pallas_call(
        filter_kernel,
        out_shape=(
            jax.ShapeDtypeStruct((TILES, NPART, C), BF16),
            jax.ShapeDtypeStruct(((TR + 1) * MW, C), F32),
            jax.ShapeDtypeStruct((REACH * MW, C), BF16),
            jax.ShapeDtypeStruct((MW, C), BF16),
        ),
        in_specs=[vmem()] * 2,
        out_specs=(vmem(),) * 4,
        scratch_shapes=[
            pltpu.VMEM((32, KDIM), F32),
            pltpu.VMEM((MW, KDIM), BF16),
            pltpu.VMEM((8 * MW, KDIM), BF16),
            pltpu.VMEM((3, (EXT + 5) * MW, C), BF16),
        ],
        compiler_params=pltpu.CompilerParams(vmem_limit_bytes=30 << 20),
        name="filter",
        cost_estimate=cost(2 * EXT * MW * KDIM * C + 18 * REACHED * C * C, 4 << 20),
    )(got, turned)


def input_kernel(own_ref, above_ref, below_ref, weight_ref, out_ref, shifted_ref):
    whole = jnp.concatenate(
        [
            above_ref[:MW].astype(F32),
            own_ref[: (REACH - 1) * MW] + above_ref[MW:].astype(F32),
            own_ref[(REACH - 1) * MW : TR * MW],
            own_ref[TR * MW :] + below_ref[...].astype(F32),
        ],
        axis=0,
    )
    for e, moved in enumerate(shifts(whole)):
        shifted_ref[e] = moved
    total = jnp.zeros((TR * MW, C), F32)
    for a in range(3):
        for e in range(3):
            total = total + lax.dot_general(
                shifted_ref[e, (2 - a) * MW : (2 - a + TR) * MW],
                weight_ref[a * 3 + e],
                (((1,), (1,)), ((), ())),
                preferred_element_type=F32,
            )
    out_ref[...] = total.astype(BF16)


def input_part(own, above, below, weight):
    return pl.pallas_call(
        input_kernel,
        out_shape=jax.ShapeDtypeStruct((TR * MW, C), BF16),
        in_specs=[vmem()] * 4,
        out_specs=vmem(),
        scratch_shapes=[pltpu.VMEM((3, (TR + 2) * MW, C), BF16)],
        compiler_params=pltpu.CompilerParams(vmem_limit_bytes=16 << 20),
        name="input",
        cost_estimate=cost(18 * TR * MW * C * C, 4 << 20),
    )(own, above, below, weight)


def sum_kernel(scale, parts_ref, out_ref):
    total = parts_ref[0].astype(F32)
    for i in range(1, parts_ref.shape[0]):
        total = total + parts_ref[i].astype(F32)
    out_ref[...] = jnp.broadcast_to((total * scale).astype(out_ref.dtype), out_ref.shape)


def sum_parts(parts, shape, dtype, scale=1.0):
    return pl.pallas_call(
        functools.partial(sum_kernel, scale),
        out_shape=jax.ShapeDtypeStruct(shape, dtype),
        in_specs=[vmem()],
        out_specs=vmem(),
        compiler_params=pltpu.CompilerParams(vmem_limit_bytes=4 << 20),
        name="sum",
        cost_estimate=cost(parts.size, parts.size * 2),
    )(parts)


def exchange(parts, axis):
    return lax.all_to_all(parts, axis, split_axis=0, concat_axis=0, tiled=True)


def body(features, weight, pool_grad, hard_index, boxes):
    grads = pool_grad[0].transpose(1, 2, 0, 3).reshape(CELLS, ROI_DEV, C)
    send = dispatch(hard_index, boxes[0].T, grads)
    up = [(t, t + 1) for t in range(TILES - 1)]
    down = [(b, a) for a, b in up]
    feature_rows = features[0].reshape(TR * MW, C)
    before = lax.ppermute(feature_rows[(TR - 1) * MW :], "tile", up)
    after = lax.ppermute(feature_rows[: REACH * MW], "tile", down)
    got = exchange(send, "tile")
    turned = turn(before, feature_rows, after)
    part, own, above, below = filter_part(got, turned)
    parts = exchange(part, "tile")
    above = lax.ppermute(above, "tile", up)
    below = lax.ppermute(below, "tile", down)
    x_grad = input_part(own, above, below, weight.reshape(9, C, C)).reshape(1, TR, MW, C)
    parts = exchange(sum_parts(parts, (4, NPART, C), BF16), "zl")
    parts = exchange(sum_parts(parts, (4, NPART, C), BF16), "zh")
    total = sum_parts(parts, (NPART, C), F32, 1.0 / IMAGES)
    total = total.reshape(9, CIN, C).transpose(1, 0, 2).reshape(CIN, 3, 3, C)
    return x_grad, total


def solution(mesh):
    split = Mesh(mesh.devices.reshape(4, 4, TILES), ("zh", "zl", "tile"))
    images = ("zh", "zl")
    return jax.shard_map(
        body,
        mesh=split,
        in_specs=(
            P(images, "tile", None, None),
            P(),
            P(images, "tile", None, None, None),
            P(images, "tile"),
            P(images, None, None),
        ),
        out_specs=(P(images, "tile", None, None), P("tile", None, None, None)),
        check_vma=False,
    )
```

```python
import functools

import jax
import jax.numpy as jnp
from jax import lax
from jax.experimental import pallas as pl
from jax.experimental.pallas import tpu as pltpu
from jax.sharding import Mesh, PartitionSpec as P

C = 256
TR = 16
MW = 64
ROI_DEV = 16
CAP = 2
REACH = 14
BINS = 7
CELLS = BINS * BINS
PROPS = 20000
TILES = 32
CHIPS = TILES // 2
IMAGES = 16
EXT = TR + REACH - 1
REACHED = 32 * MW
SLOT = CELLS + 1
BLOCK = 104
SLOTS = TILES * CAP
KDIM = TILES * BLOCK
LANES = 128
WHOLE = PROPS // LANES * LANES
F32 = jnp.float32
BF16 = jnp.bfloat16
I32 = jnp.int32
CIN = C // TILES
TILE_AXES = ("chip", "core")
NPART = 9 * CIN


def vmem():
    return pl.BlockSpec(memory_space=pltpu.VMEM)


def cost(flops, moved):
    return pl.CostEstimate(flops=flops, bytes_accessed=moved, transcendentals=0)


def iota(shape, dim):
    return lax.broadcasted_iota(I32, shape, dim)


def dispatch_kernel(
    index_hbm, boxes_hbm, grad_hbm, out_hbm, index_ref, boxes_ref, source_ref, sent_ref, sems
):
    copies = [
        pltpu.make_async_copy(index_hbm, index_ref, sems.at[0]),
        pltpu.make_async_copy(boxes_hbm, boxes_ref, sems.at[1]),
        pltpu.make_async_copy(grad_hbm, source_ref.at[:CELLS], sems.at[2]),
    ]
    for copy in copies:
        copy.start()
    copies[0].wait()
    copies[1].wait()
    lane16 = iota((4, ROI_DEV), 1)
    lanes = iota((4, LANES), 1)
    tail = jnp.concatenate(
        [boxes_ref[:, WHOLE:], jnp.zeros((4, LANES - (PROPS - WHOLE)), I32)], axis=1
    )
    chosen = jnp.zeros((4, ROI_DEV), I32)
    for r in range(ROI_DEV):
        index = index_ref[0, r]
        block = index // LANES
        at = jnp.minimum(block, WHOLE // LANES - 1) * LANES
        row = jnp.where(
            block == WHOLE // LANES, tail, boxes_ref[:, pl.ds(pl.multiple_of(at, LANES), LANES)]
        )
        found = jnp.sum(jnp.where(lanes == index - block * LANES, row, 0), axis=1, keepdims=True)
        chosen = jnp.where(lane16 == r, found, chosen)
    chosen = chosen.astype(F32)
    top = chosen[0:1]
    owner = jnp.floor(top * (1.0 / TR))
    local_top = top - owner * TR
    diag = iota((ROI_DEV, ROI_DEV), 0) == iota((ROI_DEV, ROI_DEV), 1)

    def column(row):
        wide = jnp.broadcast_to(row, (ROI_DEV, ROI_DEV))
        return jnp.sum(jnp.where(diag, wide, 0.0), axis=1, keepdims=True)

    before = iota((ROI_DEV, ROI_DEV), 0) < iota((ROI_DEV, ROI_DEV), 1)
    same = column(owner) == owner
    rank = jnp.sum(jnp.where(before & same, 1.0, 0.0), axis=0, keepdims=True)
    field = iota((ROI_DEV, C), 1)
    box_rows = jnp.zeros((ROI_DEV, C), F32)
    for f, row in enumerate((local_top, chosen[1:2], chosen[2:3], chosen[3:4])):
        box_rows = jnp.where(field == f, column(row), box_rows)
    source_ref[CELLS] = box_rows.astype(BF16)
    depth = SLOT * ROI_DEV
    wide = jnp.concatenate([owner, rank, jnp.zeros((6, ROI_DEV), F32)], axis=0).astype(BF16)
    spreading = iota((ROI_DEV, depth), 1) % ROI_DEV == iota((ROI_DEV, depth), 0)
    spread = jnp.dot(wide, spreading.astype(F32).astype(BF16), preferred_element_type=F32)
    cell = (iota((1, depth), 1) // ROI_DEV).astype(F32)
    goal = (spread[0:1] * BLOCK + spread[1:2] * SLOT + cell).astype(I32)
    copies[2].wait()
    source = source_ref[...].reshape(depth, C)
    step = KDIM // 8
    sent = []
    for m in range(8):
        part = pl.ds(m * (TILES // 8), TILES // 8)
        place = iota((step, depth), 0) == goal - m * step
        sent_ref[part] = (
            jnp.dot(place.astype(F32).astype(BF16), source, preferred_element_type=F32)
            .astype(BF16)
            .reshape(TILES // 8, BLOCK, C)
        )
        sent.append(pltpu.make_async_copy(sent_ref.at[part], out_hbm.at[part], sems.at[3 + m]))
        sent[-1].start()
    for copy in sent:
        copy.wait()


def dispatch(index, boxes_t, grads):
    return pl.pallas_call(
        dispatch_kernel,
        out_shape=jax.ShapeDtypeStruct((TILES, BLOCK, C), BF16),
        in_specs=[pl.BlockSpec(memory_space=pl.ANY)] * 3,
        out_specs=pl.BlockSpec(memory_space=pl.ANY),
        scratch_shapes=[
            pltpu.SMEM((1, ROI_DEV), I32),
            pltpu.VMEM((4, PROPS), I32),
            pltpu.VMEM((SLOT, ROI_DEV, C), BF16),
            pltpu.VMEM((TILES, BLOCK, C), BF16),
            pltpu.SemaphoreType.DMA((11,)),
        ],
        compiler_params=pltpu.CompilerParams(vmem_limit_bytes=60 << 20),
        name="dispatch",
        cost_estimate=cost(2 * KDIM * SLOT * ROI_DEV * C, 3 << 20),
    )(index, boxes_t, grads)


def weights_of(got_ref, rows_ref, cols_ref):
    slot = iota((SLOTS, KDIM), 0)
    cell = iota((SLOTS, KDIM), 1)
    first = (slot % TILES) * BLOCK + (slot // TILES) * SLOT
    box = jnp.concatenate(
        [got_ref[:, s * SLOT + CELLS, :LANES].astype(F32) for s in range(CAP)], axis=0
    )
    box = box.T[:8].astype(BF16)
    cover = ((cell >= first) & (cell < first + CELLS)).astype(F32).astype(BF16)
    field = jnp.dot(box, cover, preferred_element_type=F32).astype(I32)
    within = iota((1, KDIM), 1) % BLOCK
    inside = within < CAP * SLOT
    within = within % SLOT
    inside = inside & (within < CELLS)
    row_bin = within // BINS
    col_bin = within - row_bin * BINS
    row = jnp.where(inside, field[0:1] + row_bin * field[2:3], -9)
    col = field[1:2] + col_bin * field[3:4]
    grid = iota((32, KDIM), 0)
    rows_ref[...] = jnp.where(grid == row, 0.75, jnp.where(grid == row + 1, 0.25, 0.0))
    grid = iota((MW, KDIM), 0)
    cols_ref[...] = jnp.where(grid == col, 0.25, jnp.where(grid == col + 1, 0.75, 0.0)).astype(BF16)


def rows_of(start, count, got_ref, rows_ref, cols_ref, left_ref):
    cols = cols_ref[...]
    for h in range(count):
        left_ref[h * MW : (h + 1) * MW] = cols * rows_ref[start + h : start + h + 1, :].astype(BF16)
    return jnp.dot(
        left_ref[: count * MW], got_ref[...].reshape(KDIM, C), preferred_element_type=F32
    )


def turn_kernel(before_ref, own_ref, after_ref, out_ref):
    rows = jnp.concatenate(
        [before_ref[...], own_ref[...], after_ref[...], jnp.zeros((MW, C), BF16)], axis=0
    )
    out_ref[...] = rows.T


def turn(before, own, after):
    return pl.pallas_call(
        turn_kernel,
        out_shape=jax.ShapeDtypeStruct((C, REACHED), BF16),
        in_specs=[vmem()] * 3,
        out_specs=vmem(),
        compiler_params=pltpu.CompilerParams(vmem_limit_bytes=8 << 20),
        name="turn",
        cost_estimate=cost(TR * MW * C, 2 << 20),
    )(before, own, after)


def shifts(rows):
    count = rows.shape[0]
    column = iota((count, C), 0) % MW
    return (
        jnp.where(column == MW - 1, 0.0, pltpu.roll(rows, count - 1, 0)).astype(BF16),
        rows.astype(BF16),
        jnp.where(column == 0, 0.0, pltpu.roll(rows, 1, 0)).astype(BF16),
    )


def filter_kernel(
    core_ref, got_ref, turned_ref, keep_ref, give_ref, own_ref, above_ref, below_ref,
    rows_ref, cols_ref, left_ref, shifted_ref,
):
    weights_of(got_ref, rows_ref, cols_ref)
    shifted_ref[:, : 2 * MW] = jnp.zeros((3, 2 * MW, C), BF16)
    shifted_ref[:, (2 + EXT) * MW :] = jnp.zeros((3, 3 * MW, C), BF16)
    for start, count in ((0, 8), (8, 8), (16, 8), (24, 5)):
        part = rows_of(start, count, got_ref, rows_ref, cols_ref, left_ref)
        for e, moved in enumerate(shifts(part)):
            shifted_ref[e, (2 + start) * MW : (2 + start + count) * MW] = moved
        if start < TR:
            own_ref[start * MW : (start + count) * MW] = part
        if start == 0:
            below_ref[...] = part[:MW].astype(BF16)
        if start == 8:
            above_ref[:MW] = part[7 * MW :].astype(BF16)
        if start == 16:
            own_ref[TR * MW :] = part[:MW]
            above_ref[MW : 9 * MW] = part.astype(BF16)
        if start == 24:
            above_ref[9 * MW :] = part.astype(BF16)
    first = core_ref[0] == 0
    for a in range(3):
        for e in range(3):
            part = jnp.dot(
                turned_ref[...],
                shifted_ref[e, (2 - a) * MW : (2 - a) * MW + REACHED],
                preferred_element_type=F32,
            )
            part = part.reshape(CHIPS, 2, CIN, C)
            at = (a * 3 + e) * CIN
            keep_ref[:, at : at + CIN, :] = jnp.where(first, part[:, 0], part[:, 1])
            give_ref[:, at : at + CIN, :] = jnp.where(first, part[:, 1], part[:, 0]).astype(BF16)


def filter_part(core, got, turned):
    return pl.pallas_call(
        filter_kernel,
        out_shape=(
            jax.ShapeDtypeStruct((CHIPS, NPART, C), F32),
            jax.ShapeDtypeStruct((CHIPS, NPART, C), BF16),
            jax.ShapeDtypeStruct(((TR + 1) * MW, C), F32),
            jax.ShapeDtypeStruct((REACH * MW, C), BF16),
            jax.ShapeDtypeStruct((MW, C), BF16),
        ),
        in_specs=[pl.BlockSpec(memory_space=pltpu.SMEM), vmem(), vmem()],
        out_specs=(vmem(),) * 5,
        scratch_shapes=[
            pltpu.VMEM((32, KDIM), F32),
            pltpu.VMEM((MW, KDIM), BF16),
            pltpu.VMEM((8 * MW, KDIM), BF16),
            pltpu.VMEM((3, (EXT + 5) * MW, C), BF16),
        ],
        compiler_params=pltpu.CompilerParams(vmem_limit_bytes=30 << 20),
        name="filter",
        cost_estimate=cost(2 * EXT * MW * KDIM * C + 18 * REACHED * C * C, 4 << 20),
    )(core, got, turned)


def input_kernel(own_ref, above_ref, below_ref, weight_ref, out_ref, shifted_ref):
    whole = jnp.concatenate(
        [
            above_ref[:MW].astype(F32),
            own_ref[: (REACH - 1) * MW] + above_ref[MW:].astype(F32),
            own_ref[(REACH - 1) * MW : TR * MW],
            own_ref[TR * MW :] + below_ref[...].astype(F32),
        ],
        axis=0,
    )
    for e, moved in enumerate(shifts(whole)):
        shifted_ref[e] = moved
    total = jnp.zeros((TR * MW, C), F32)
    for a in range(3):
        for e in range(3):
            total = total + lax.dot_general(
                shifted_ref[e, (2 - a) * MW : (2 - a + TR) * MW],
                weight_ref[a * 3 + e],
                (((1,), (1,)), ((), ())),
                preferred_element_type=F32,
            )
    out_ref[...] = total.astype(BF16)


def input_part(own, above, below, weight):
    return pl.pallas_call(
        input_kernel,
        out_shape=jax.ShapeDtypeStruct((TR * MW, C), BF16),
        in_specs=[vmem()] * 4,
        out_specs=vmem(),
        scratch_shapes=[pltpu.VMEM((3, (TR + 2) * MW, C), BF16)],
        compiler_params=pltpu.CompilerParams(vmem_limit_bytes=16 << 20),
        name="input",
        cost_estimate=cost(18 * TR * MW * C * C, 4 << 20),
    )(own, above, below, weight)


def sum_kernel(scale, parts_ref, out_ref):
    total = parts_ref[0].astype(F32)
    for i in range(1, parts_ref.shape[0]):
        total = total + parts_ref[i].astype(F32)
    out_ref[...] = jnp.broadcast_to((total * scale).astype(out_ref.dtype), out_ref.shape)


def sum_parts(parts, shape, dtype, scale=1.0):
    return pl.pallas_call(
        functools.partial(sum_kernel, scale),
        out_shape=jax.ShapeDtypeStruct(shape, dtype),
        in_specs=[vmem()],
        out_specs=vmem(),
        compiler_params=pltpu.CompilerParams(vmem_limit_bytes=4 << 20),
        name="sum",
        cost_estimate=cost(parts.size, parts.size * 2),
    )(parts)


def pair_kernel(keep_ref, got_ref, out_ref):
    out_ref[...] = (keep_ref[...] + got_ref[...].astype(F32)).astype(BF16)


def sum_pair(keep, got):
    return pl.pallas_call(
        pair_kernel,
        out_shape=jax.ShapeDtypeStruct(keep.shape, BF16),
        in_specs=[vmem()] * 2,
        out_specs=vmem(),
        compiler_params=pltpu.CompilerParams(vmem_limit_bytes=4 << 20),
        name="pair",
        cost_estimate=cost(keep.size, keep.size * 8),
    )(keep, got)


def exchange(parts, axis):
    return lax.all_to_all(parts, axis, split_axis=0, concat_axis=0, tiled=True)


def body(features, weight, pool_grad, hard_index, boxes):
    grads = pool_grad[0].transpose(1, 2, 0, 3).reshape(CELLS, ROI_DEV, C)
    send = dispatch(hard_index, boxes[0].T, grads)
    up = [(t, t + 1) for t in range(TILES - 1)]
    down = [(b, a) for a, b in up]
    feature_rows = features[0].reshape(TR * MW, C)
    before = lax.ppermute(feature_rows[(TR - 1) * MW :], TILE_AXES, up)
    after = lax.ppermute(feature_rows[: REACH * MW], TILE_AXES, down)
    got = exchange(send, TILE_AXES)
    turned = turn(before, feature_rows, after)
    core = lax.axis_index("core").reshape(1)
    keep, give, own, above, below = filter_part(core, got, turned)
    taken = lax.ppermute(give, "core", [(0, 1), (1, 0)])
    parts = exchange(sum_pair(keep, taken), "chip")
    above = lax.ppermute(above, TILE_AXES, up)
    below = lax.ppermute(below, TILE_AXES, down)
    x_grad = input_part(own, above, below, weight.reshape(9, C, C)).reshape(1, TR, MW, C)
    parts = exchange(sum_parts(parts, (4, NPART, C), BF16), "zl")
    parts = sum_parts(parts, (1, NPART, C), BF16)
    parts = lax.all_gather(parts, "zh", tiled=True, axis_index_groups=[[0, 1], [2, 3]])
    parts = sum_parts(parts, (1, NPART, C), BF16)
    parts = lax.all_gather(parts, "zh", tiled=True, axis_index_groups=[[0, 3], [1, 2]])
    total = sum_parts(parts, (NPART, C), F32, 1.0 / IMAGES)
    total = total.reshape(9, CIN, C).transpose(1, 0, 2).reshape(CIN, 3, 3, C)
    return x_grad, total


def solution(mesh):
    split = Mesh(mesh.devices.reshape(4, 4, CHIPS, 2), ("zh", "zl", "chip", "core"))
    images = ("zh", "zl")
    return jax.shard_map(
        body,
        mesh=split,
        in_specs=(
            P(images, TILE_AXES, None, None),
            P(),
            P(images, TILE_AXES, None, None, None),
            P(images, TILE_AXES),
            P(images, None, None),
        ),
        out_specs=(P(images, TILE_AXES, None, None), P(TILE_AXES, None, None, None)),
        check_vma=False,
    )
```

```python
import functools

import jax
import jax.numpy as jnp
from jax import lax
from jax.experimental import pallas as pl
from jax.experimental.pallas import tpu as pltpu
from jax.sharding import Mesh, PartitionSpec as P

C = 256
TR = 16
MW = 64
ROI_DEV = 16
CAP = 2
REACH = 14
BINS = 7
CELLS = BINS * BINS
PROPS = 20000
TILES = 32
CHIPS = TILES // 2
IMAGES = 16
EXT = TR + REACH - 1
SLOT = CELLS + 1
BLOCK = 104
SLOTS = TILES * CAP
KDIM = TILES * BLOCK
LANES = 128
WHOLE = PROPS // LANES * LANES
F32 = jnp.float32
BF16 = jnp.bfloat16
I32 = jnp.int32
CIN = C // TILES
TILE_AXES = ("chip", "core")
NPART = 9 * CIN


def vmem():
    return pl.BlockSpec(memory_space=pltpu.VMEM)


def hbm():
    return pl.BlockSpec(memory_space=pltpu.HBM)


def cost(flops, moved):
    return pl.CostEstimate(flops=flops, bytes_accessed=moved, transcendentals=0)


def iota(shape, dim):
    return lax.broadcasted_iota(I32, shape, dim)


def dispatch_kernel(
    index_hbm, boxes_hbm, grad_hbm, out_hbm, index_ref, boxes_ref, source_ref, sent_ref, sems
):
    copies = [
        pltpu.make_async_copy(index_hbm, index_ref, sems.at[0]),
        pltpu.make_async_copy(boxes_hbm, boxes_ref, sems.at[1]),
        pltpu.make_async_copy(grad_hbm, source_ref.at[:CELLS], sems.at[2]),
    ]
    for copy in copies:
        copy.start()
    copies[0].wait()
    copies[1].wait()
    lane16 = iota((4, ROI_DEV), 1)
    lanes = iota((4, LANES), 1)
    tail = jnp.concatenate(
        [boxes_ref[:, WHOLE:], jnp.zeros((4, LANES - (PROPS - WHOLE)), I32)], axis=1
    )
    chosen = jnp.zeros((4, ROI_DEV), I32)
    for r in range(ROI_DEV):
        index = index_ref[0, r]
        block = index // LANES
        at = jnp.minimum(block, WHOLE // LANES - 1) * LANES
        row = jnp.where(
            block == WHOLE // LANES, tail, boxes_ref[:, pl.ds(pl.multiple_of(at, LANES), LANES)]
        )
        found = jnp.sum(jnp.where(lanes == index - block * LANES, row, 0), axis=1, keepdims=True)
        chosen = jnp.where(lane16 == r, found, chosen)
    chosen = chosen.astype(F32)
    top = chosen[0:1]
    owner = jnp.floor(top * (1.0 / TR))
    local_top = top - owner * TR
    diag = iota((ROI_DEV, ROI_DEV), 0) == iota((ROI_DEV, ROI_DEV), 1)

    def column(row):
        wide = jnp.broadcast_to(row, (ROI_DEV, ROI_DEV))
        return jnp.sum(jnp.where(diag, wide, 0.0), axis=1, keepdims=True)

    before = iota((ROI_DEV, ROI_DEV), 0) < iota((ROI_DEV, ROI_DEV), 1)
    same = column(owner) == owner
    rank = jnp.sum(jnp.where(before & same, 1.0, 0.0), axis=0, keepdims=True)
    field = iota((ROI_DEV, C), 1)
    box_rows = jnp.zeros((ROI_DEV, C), F32)
    for f, row in enumerate((local_top, chosen[1:2], chosen[2:3], chosen[3:4])):
        box_rows = jnp.where(field == f, column(row), box_rows)
    source_ref[CELLS] = box_rows.astype(BF16)
    depth = SLOT * ROI_DEV
    wide = jnp.concatenate([owner, rank, jnp.zeros((6, ROI_DEV), F32)], axis=0).astype(BF16)
    spreading = iota((ROI_DEV, depth), 1) % ROI_DEV == iota((ROI_DEV, depth), 0)
    spread = jnp.dot(wide, spreading.astype(F32).astype(BF16), preferred_element_type=F32)
    cell = (iota((1, depth), 1) // ROI_DEV).astype(F32)
    goal = (spread[0:1] * BLOCK + spread[1:2] * SLOT + cell).astype(I32)
    copies[2].wait()
    source = source_ref[...].reshape(depth, C)
    step = KDIM // 8
    sent = []
    for m in range(8):
        part = pl.ds(m * (TILES // 8), TILES // 8)
        place = iota((step, depth), 0) == goal - m * step
        sent_ref[part] = (
            jnp.dot(place.astype(F32).astype(BF16), source, preferred_element_type=F32)
            .astype(BF16)
            .reshape(TILES // 8, BLOCK, C)
        )
        sent.append(pltpu.make_async_copy(sent_ref.at[part], out_hbm.at[part], sems.at[3 + m]))
        sent[-1].start()
    for copy in sent:
        copy.wait()


def dispatch(index, boxes_t, grads):
    return pl.pallas_call(
        dispatch_kernel,
        out_shape=jax.ShapeDtypeStruct((TILES, BLOCK, C), BF16),
        in_specs=[pl.BlockSpec(memory_space=pl.ANY)] * 3,
        out_specs=pl.BlockSpec(memory_space=pl.ANY),
        scratch_shapes=[
            pltpu.SMEM((1, ROI_DEV), I32),
            pltpu.VMEM((4, PROPS), I32),
            pltpu.VMEM((SLOT, ROI_DEV, C), BF16),
            pltpu.VMEM((TILES, BLOCK, C), BF16),
            pltpu.SemaphoreType.DMA((11,)),
        ],
        compiler_params=pltpu.CompilerParams(vmem_limit_bytes=60 << 20),
        name="dispatch",
        cost_estimate=cost(2 * KDIM * SLOT * ROI_DEV * C, 3 << 20),
    )(*(pltpu.with_memory_space_constraint(x, pltpu.HBM) for x in (index, boxes_t, grads)))


def weights_of(got_ref, rows_ref, cols_ref):
    slot = iota((SLOTS, KDIM), 0)
    cell = iota((SLOTS, KDIM), 1)
    first = (slot % TILES) * BLOCK + (slot // TILES) * SLOT
    box = jnp.concatenate(
        [got_ref[:, s * SLOT + CELLS, :LANES].astype(F32) for s in range(CAP)], axis=0
    )
    box = box.T[:8].astype(BF16)
    cover = ((cell >= first) & (cell < first + CELLS)).astype(F32).astype(BF16)
    field = jnp.dot(box, cover, preferred_element_type=F32).astype(I32)
    within = iota((1, KDIM), 1) % BLOCK
    inside = within < CAP * SLOT
    within = within % SLOT
    inside = inside & (within < CELLS)
    row_bin = within // BINS
    col_bin = within - row_bin * BINS
    row = jnp.where(inside, field[0:1] + row_bin * field[2:3], -9)
    col = field[1:2] + col_bin * field[3:4]
    grid = iota((32, KDIM), 0)
    rows_ref[...] = jnp.where(grid == row, 0.75, jnp.where(grid == row + 1, 0.25, 0.0))
    grid = iota((MW, KDIM), 0)
    cols_ref[...] = jnp.where(grid == col, 0.25, jnp.where(grid == col + 1, 0.75, 0.0)).astype(BF16)


def rows_of(start, count, got_ref, rows_ref, cols_ref, left_ref):
    cols = cols_ref[...]
    for h in range(count):
        left_ref[h * MW : (h + 1) * MW] = cols * rows_ref[start + h : start + h + 1, :].astype(BF16)
    return jnp.dot(
        left_ref[: count * MW], got_ref[...].reshape(KDIM, C), preferred_element_type=F32
    )


def shifts(rows, before, after):
    count = rows.shape[0]
    column = iota((count, C), 0) % MW
    one_less = jnp.where(column == 0, 0.0, pltpu.roll(rows, 1, 0)).astype(BF16)
    one_more = jnp.where(column == MW - 1, 0.0, pltpu.roll(rows, count - 1, 0)).astype(BF16)
    return {before: one_less, 1: rows.astype(BF16), after: one_more}


def turn_rows(rows, out_ref):
    for e, moved in shifts(rows.astype(F32), 0, 2).items():
        out_ref[e * C : (e + 1) * C] = moved.T


def turn_kernel(rows_ref, out_hbm, out_ref, sem):
    turn_rows(rows_ref[...], out_ref)
    copy = pltpu.make_async_copy(out_ref, out_hbm, sem)
    copy.start()
    copy.wait()


def turn(rows):
    return pl.pallas_call(
        turn_kernel,
        out_shape=pltpu.HBM((3 * C, TR * MW), BF16),
        in_specs=[vmem()],
        out_specs=hbm(),
        scratch_shapes=[pltpu.VMEM((3 * C, TR * MW), BF16), pltpu.SemaphoreType.DMA],
        compiler_params=pltpu.CompilerParams(vmem_limit_bytes=12 << 20),
        name="turn",
        cost_estimate=cost(TR * MW * C, 2 << 20),
    )(rows)


def filter_kernel(
    core_ref, got_ref, turned_hbm, before_ref, after_ref,
    keep_ref, give_ref, own_hbm, above_ref, below_ref,
    rows_ref, cols_ref, left_ref, map_ref, turned_ref, rest_ref, own_ref, sems,
):
    fetch = pltpu.make_async_copy(turned_hbm, turned_ref, sems.at[0])
    fetch.start()
    weights_of(got_ref, rows_ref, cols_ref)
    fetch.wait()
    rest = jnp.concatenate([after_ref[...], before_ref[...], jnp.zeros((MW, C), BF16)], axis=0)
    turn_rows(rest, rest_ref)
    map_ref[: 2 * MW] = jnp.zeros((2 * MW, C), BF16)
    map_ref[(2 + EXT) * MW :] = jnp.zeros((4 * MW, C), BF16)
    for start, count in ((0, 8), (8, 8), (16, 8), (24, 5)):
        part = rows_of(start, count, got_ref, rows_ref, cols_ref, left_ref)
        map_ref[(2 + start) * MW : (2 + start + count) * MW] = part.astype(BF16)
        if start < TR:
            own_ref[start * MW : (start + count) * MW] = part
        if start == 0:
            below_ref[...] = part[:MW].astype(BF16)
            map_ref[(4 + EXT) * MW : (5 + EXT) * MW] = part[:MW].astype(BF16)
        if start == 8:
            above_ref[:MW] = part[7 * MW :].astype(BF16)
        if start == 16:
            own_ref[TR * MW :] = part[:MW]
            above_ref[MW : 9 * MW] = part.astype(BF16)
        if start == 24:
            above_ref[9 * MW :] = part.astype(BF16)
    put = pltpu.make_async_copy(own_ref, own_hbm, sems.at[1])
    put.start()
    first = core_ref[0] == 0
    for a in range(3):
        part = jnp.dot(
            turned_ref[...],
            map_ref[(3 - a) * MW : (3 - a + TR) * MW],
            preferred_element_type=F32,
        ) + jnp.dot(
            rest_ref[...],
            map_ref[(3 - a + TR) * MW : (3 - a + 2 * TR) * MW],
            preferred_element_type=F32,
        )
        part = part.reshape(3, CHIPS, 2, CIN, C)
        for e in range(3):
            at = (a * 3 + e) * CIN
            keep_ref[:, at : at + CIN, :] = jnp.where(first, part[e, :, 0], part[e, :, 1])
            give_ref[:, at : at + CIN, :] = jnp.where(first, part[e, :, 1], part[e, :, 0]).astype(BF16)
    put.wait()


def filter_part(core, got, turned, before, after):
    return pl.pallas_call(
        filter_kernel,
        out_shape=(
            jax.ShapeDtypeStruct((CHIPS, NPART, C), F32),
            jax.ShapeDtypeStruct((CHIPS, NPART, C), BF16),
            pltpu.HBM(((TR + 1) * MW, C), F32),
            jax.ShapeDtypeStruct((REACH * MW, C), BF16),
            jax.ShapeDtypeStruct((MW, C), BF16),
        ),
        in_specs=[pl.BlockSpec(memory_space=pltpu.SMEM), vmem(), hbm(), vmem(), vmem()],
        out_specs=(vmem(), vmem(), hbm(), vmem(), vmem()),
        scratch_shapes=[
            pltpu.VMEM((32, KDIM), F32),
            pltpu.VMEM((MW, KDIM), BF16),
            pltpu.VMEM((8 * MW, KDIM), BF16),
            pltpu.VMEM(((EXT + 6) * MW, C), BF16),
            pltpu.VMEM((3 * C, TR * MW), BF16),
            pltpu.VMEM((3 * C, TR * MW), BF16),
            pltpu.VMEM(((TR + 1) * MW, C), F32),
            pltpu.SemaphoreType.DMA((2,)),
        ],
        compiler_params=pltpu.CompilerParams(vmem_limit_bytes=30 << 20),
        name="filter",
        cost_estimate=cost(2 * EXT * MW * KDIM * C + 36 * TR * MW * C * C, 4 << 20),
    )(core, got, pltpu.with_memory_space_constraint(turned, pltpu.HBM), before, after)


def input_kernel(own_ref, above_ref, below_ref, weight_ref, out_ref, shifted_ref):
    whole = jnp.concatenate(
        [
            above_ref[:MW].astype(F32),
            own_ref[: (REACH - 1) * MW] + above_ref[MW:].astype(F32),
            own_ref[(REACH - 1) * MW : TR * MW],
            own_ref[TR * MW :] + below_ref[...].astype(F32),
        ],
        axis=0,
    )
    for e, moved in shifts(whole, 2, 0).items():
        shifted_ref[e] = moved
    total = jnp.zeros((TR * MW, C), F32)
    for a in range(3):
        for e in range(3):
            total = total + lax.dot_general(
                shifted_ref[e, (2 - a) * MW : (2 - a + TR) * MW],
                weight_ref[a * 3 + e],
                (((1,), (1,)), ((), ())),
                preferred_element_type=F32,
            )
    out_ref[...] = total.astype(BF16)


def input_part(own, above, below, weight):
    return pl.pallas_call(
        input_kernel,
        out_shape=jax.ShapeDtypeStruct((TR * MW, C), BF16),
        in_specs=[vmem()] * 4,
        out_specs=vmem(),
        scratch_shapes=[pltpu.VMEM((3, (TR + 2) * MW, C), BF16)],
        compiler_params=pltpu.CompilerParams(vmem_limit_bytes=16 << 20),
        name="input",
        cost_estimate=cost(18 * TR * MW * C * C, 4 << 20),
    )(own, above, below, weight)


def sum_kernel(scale, parts_ref, out_ref):
    total = parts_ref[0].astype(F32)
    for i in range(1, parts_ref.shape[0]):
        total = total + parts_ref[i].astype(F32)
    out_ref[...] = jnp.broadcast_to((total * scale).astype(out_ref.dtype), out_ref.shape)


def sum_parts(parts, shape, dtype, scale=1.0):
    return pl.pallas_call(
        functools.partial(sum_kernel, scale),
        out_shape=jax.ShapeDtypeStruct(shape, dtype),
        in_specs=[vmem()],
        out_specs=vmem(),
        compiler_params=pltpu.CompilerParams(vmem_limit_bytes=4 << 20),
        name="sum",
        cost_estimate=cost(parts.size, parts.size * 2),
    )(parts)


def pair_kernel(keep_ref, got_ref, out_ref):
    out_ref[...] = (keep_ref[...].astype(F32) + got_ref[...].astype(F32)).astype(BF16)


def sum_pair(keep, got):
    return pl.pallas_call(
        pair_kernel,
        out_shape=jax.ShapeDtypeStruct(keep.shape, BF16),
        in_specs=[vmem()] * 2,
        out_specs=vmem(),
        compiler_params=pltpu.CompilerParams(vmem_limit_bytes=4 << 20),
        name="pair",
        cost_estimate=cost(keep.size, keep.size * 8),
    )(keep, got)


def exchange(parts, axis):
    return lax.all_to_all(parts, axis, split_axis=0, concat_axis=0, tiled=True)


def body(features, weight, pool_grad, hard_index, boxes):
    grads = pool_grad[0].transpose(1, 2, 0, 3).reshape(CELLS, ROI_DEV, C)
    send = dispatch(hard_index, boxes[0].T, grads)
    up = [(t, t + 1) for t in range(TILES - 1)]
    down = [(b, a) for a, b in up]
    feature_rows = features[0].reshape(TR * MW, C)
    before = lax.ppermute(feature_rows[(TR - 1) * MW :], TILE_AXES, up)
    after = lax.ppermute(feature_rows[: REACH * MW], TILE_AXES, down)
    got = exchange(send, TILE_AXES)
    turned = turn(feature_rows)
    core = lax.axis_index("core").reshape(1)
    keep, give, own, above, below = filter_part(core, got, turned, before, after)
    taken = lax.ppermute(give, "core", [(0, 1), (1, 0)])
    parts = exchange(sum_pair(keep, taken), "chip")
    above = lax.ppermute(above, TILE_AXES, up)
    below = lax.ppermute(below, TILE_AXES, down)
    x_grad = input_part(own, above, below, weight.reshape(9, C, C)).reshape(1, TR, MW, C)
    parts = exchange(sum_parts(parts, (4, NPART, C), BF16), "zl")
    parts = sum_parts(parts, (NPART, C), BF16)
    taken = lax.ppermute(parts, "zh", [(0, 1), (1, 0), (2, 3), (3, 2)])
    parts = sum_pair(parts, taken)
    parts, x_grad = lax.optimization_barrier((parts, x_grad))
    parts = lax.all_gather(parts[None], "zh", tiled=True, axis_index_groups=[[0, 3], [1, 2]])
    total = sum_parts(parts, (NPART, C), F32, 1.0 / IMAGES)
    total = total.reshape(9, CIN, C).transpose(1, 0, 2).reshape(CIN, 3, 3, C)
    return x_grad, total


def solution(mesh):
    split = Mesh(mesh.devices.reshape(4, 4, CHIPS, 2), ("zh", "zl", "chip", "core"))
    images = ("zh", "zl")
    return jax.shard_map(
        body,
        mesh=split,
        in_specs=(
            P(images, TILE_AXES, None, None),
            P(),
            P(images, TILE_AXES, None, None, None),
            P(images, TILE_AXES),
            P(images, None, None),
        ),
        out_specs=(P(images, TILE_AXES, None, None), P(TILE_AXES, None, None, None)),
        check_vma=False,
    )
```

```python
import functools

import jax
import jax.numpy as jnp
from jax import lax
from jax.experimental import pallas as pl
from jax.experimental.pallas import tpu as pltpu
from jax.sharding import Mesh, PartitionSpec as P

C = 256
TR = 16
MW = 64
ROI_DEV = 16
CAP = 2
REACH = 14
BINS = 7
CELLS = BINS * BINS
PROPS = 20000
TILES = 32
CHIPS = TILES // 2
IMAGES = 16
EXT = TR + REACH - 1
SLOT = CELLS + 1
BLOCK = 104
SLOTS = TILES * CAP
KDIM = TILES * BLOCK
LANES = 128
WHOLE = PROPS // LANES * LANES
F32 = jnp.float32
BF16 = jnp.bfloat16
I32 = jnp.int32
CIN = C // TILES
TILE_AXES = ("chip", "core")
NPART = 9 * CIN


def vmem():
    return pl.BlockSpec(memory_space=pltpu.VMEM)


def hbm():
    return pl.BlockSpec(memory_space=pltpu.HBM)


def cost(flops, moved):
    return pl.CostEstimate(flops=flops, bytes_accessed=moved, transcendentals=0)


def iota(shape, dim):
    return lax.broadcasted_iota(I32, shape, dim)


def dispatch_kernel(
    index_hbm, boxes_hbm, grad_hbm, out_hbm, index_ref, boxes_ref, source_ref, sent_ref, sems
):
    copies = [
        pltpu.make_async_copy(index_hbm, index_ref, sems.at[0]),
        pltpu.make_async_copy(boxes_hbm, boxes_ref, sems.at[1]),
        pltpu.make_async_copy(grad_hbm, source_ref.at[:CELLS], sems.at[2]),
    ]
    for copy in copies:
        copy.start()
    copies[0].wait()
    copies[1].wait()
    lane16 = iota((4, ROI_DEV), 1)
    lanes = iota((4, LANES), 1)
    tail = jnp.concatenate(
        [boxes_ref[:, WHOLE:], jnp.zeros((4, LANES - (PROPS - WHOLE)), I32)], axis=1
    )
    chosen = jnp.zeros((4, ROI_DEV), I32)
    for r in range(ROI_DEV):
        index = index_ref[0, r]
        block = index // LANES
        at = jnp.minimum(block, WHOLE // LANES - 1) * LANES
        row = jnp.where(
            block == WHOLE // LANES, tail, boxes_ref[:, pl.ds(pl.multiple_of(at, LANES), LANES)]
        )
        found = jnp.sum(jnp.where(lanes == index - block * LANES, row, 0), axis=1, keepdims=True)
        chosen = jnp.where(lane16 == r, found, chosen)
    chosen = chosen.astype(F32)
    top = chosen[0:1]
    owner = jnp.floor(top * (1.0 / TR))
    local_top = top - owner * TR
    diag = iota((ROI_DEV, ROI_DEV), 0) == iota((ROI_DEV, ROI_DEV), 1)

    def column(row):
        wide = jnp.broadcast_to(row, (ROI_DEV, ROI_DEV))
        return jnp.sum(jnp.where(diag, wide, 0.0), axis=1, keepdims=True)

    before = iota((ROI_DEV, ROI_DEV), 0) < iota((ROI_DEV, ROI_DEV), 1)
    same = column(owner) == owner
    rank = jnp.sum(jnp.where(before & same, 1.0, 0.0), axis=0, keepdims=True)
    field = iota((ROI_DEV, C), 1)
    box_rows = jnp.zeros((ROI_DEV, C), F32)
    for f, row in enumerate((local_top, chosen[1:2], chosen[2:3], chosen[3:4])):
        box_rows = jnp.where(field == f, column(row), box_rows)
    source_ref[CELLS] = box_rows.astype(BF16)
    depth = SLOT * ROI_DEV
    wide = jnp.concatenate([owner, rank, jnp.zeros((6, ROI_DEV), F32)], axis=0).astype(BF16)
    spreading = iota((ROI_DEV, depth), 1) % ROI_DEV == iota((ROI_DEV, depth), 0)
    spread = jnp.dot(wide, spreading.astype(F32).astype(BF16), preferred_element_type=F32)
    cell = (iota((1, depth), 1) // ROI_DEV).astype(F32)
    goal = (spread[0:1] * BLOCK + spread[1:2] * SLOT + cell).astype(I32)
    copies[2].wait()
    source = source_ref[...].reshape(depth, C)
    step = KDIM // 8
    sent = []
    for m in range(8):
        part = pl.ds(m * (TILES // 8), TILES // 8)
        place = iota((step, depth), 0) == goal - m * step
        sent_ref[part] = (
            jnp.dot(place.astype(F32).astype(BF16), source, preferred_element_type=F32)
            .astype(BF16)
            .reshape(TILES // 8, BLOCK, C)
        )
        sent.append(pltpu.make_async_copy(sent_ref.at[part], out_hbm.at[part], sems.at[3 + m]))
        sent[-1].start()
    for copy in sent:
        copy.wait()


def dispatch(index, boxes_t, grads):
    return pl.pallas_call(
        dispatch_kernel,
        out_shape=jax.ShapeDtypeStruct((TILES, BLOCK, C), BF16),
        in_specs=[pl.BlockSpec(memory_space=pl.ANY)] * 3,
        out_specs=pl.BlockSpec(memory_space=pl.ANY),
        scratch_shapes=[
            pltpu.SMEM((1, ROI_DEV), I32),
            pltpu.VMEM((4, PROPS), I32),
            pltpu.VMEM((SLOT, ROI_DEV, C), BF16),
            pltpu.VMEM((TILES, BLOCK, C), BF16),
            pltpu.SemaphoreType.DMA((11,)),
        ],
        compiler_params=pltpu.CompilerParams(vmem_limit_bytes=60 << 20),
        name="dispatch",
        cost_estimate=cost(2 * KDIM * SLOT * ROI_DEV * C, 3 << 20),
    )(*(pltpu.with_memory_space_constraint(x, pltpu.HBM) for x in (index, boxes_t, grads)))


def weights_of(got_ref, rows_ref, cols_ref):
    slot = iota((SLOTS, KDIM), 0)
    cell = iota((SLOTS, KDIM), 1)
    first = (slot % TILES) * BLOCK + (slot // TILES) * SLOT
    box = jnp.concatenate(
        [got_ref[:, s * SLOT + CELLS, :LANES].astype(F32) for s in range(CAP)], axis=0
    )
    box = box.T[:8].astype(BF16)
    cover = ((cell >= first) & (cell < first + CELLS)).astype(F32).astype(BF16)
    field = jnp.dot(box, cover, preferred_element_type=F32).astype(I32)
    within = iota((1, KDIM), 1) % BLOCK
    inside = within < CAP * SLOT
    within = within % SLOT
    inside = inside & (within < CELLS)
    row_bin = within // BINS
    col_bin = within - row_bin * BINS
    row = jnp.where(inside, field[0:1] + row_bin * field[2:3], -9)
    col = field[1:2] + col_bin * field[3:4]
    grid = iota((32, KDIM), 0)
    rows_ref[...] = jnp.where(grid == row, 0.75, jnp.where(grid == row + 1, 0.25, 0.0))
    grid = iota((MW, KDIM), 0)
    cols_ref[...] = jnp.where(grid == col, 0.25, jnp.where(grid == col + 1, 0.75, 0.0)).astype(BF16)


def rows_of(start, count, got_ref, rows_ref, cols_ref, left_ref):
    cols = cols_ref[...]
    for h in range(count):
        left_ref[h * MW : (h + 1) * MW] = cols * rows_ref[start + h : start + h + 1, :].astype(BF16)
    return jnp.dot(
        left_ref[: count * MW], got_ref[...].reshape(KDIM, C), preferred_element_type=F32
    )


def shifts(rows, before, after):
    count = rows.shape[0]
    column = iota((count, C), 0) % MW
    one_less = jnp.where(column == 0, 0.0, pltpu.roll(rows, 1, 0)).astype(BF16)
    one_more = jnp.where(column == MW - 1, 0.0, pltpu.roll(rows, count - 1, 0)).astype(BF16)
    return {before: one_less, 1: rows.astype(BF16), after: one_more}


def turn_rows(rows, out_ref):
    for e, moved in shifts(rows.astype(F32), 0, 2).items():
        out_ref[e * C : (e + 1) * C] = moved.T


def filter_kernel(
    core_ref, got_ref, features_ref, before_ref, after_ref,
    keep_ref, give_ref, own_hbm, above_ref, below_ref,
    rows_ref, cols_ref, left_ref, map_ref, turned_ref, own_ref, sem,
):
    weights_of(got_ref, rows_ref, cols_ref)
    features = jnp.concatenate(
        [features_ref[...], after_ref[...], before_ref[...], jnp.zeros((MW, C), BF16)], axis=0
    )
    turn_rows(features, turned_ref)
    map_ref[: 2 * MW] = jnp.zeros((2 * MW, C), BF16)
    map_ref[(2 + EXT) * MW :] = jnp.zeros((4 * MW, C), BF16)
    for start, count in ((0, 8), (8, 8), (16, 8), (24, 5)):
        part = rows_of(start, count, got_ref, rows_ref, cols_ref, left_ref)
        map_ref[(2 + start) * MW : (2 + start + count) * MW] = part.astype(BF16)
        if start < TR:
            own_ref[start * MW : (start + count) * MW] = part
        if start == 0:
            below_ref[...] = part[:MW].astype(BF16)
            map_ref[(4 + EXT) * MW : (5 + EXT) * MW] = part[:MW].astype(BF16)
        if start == 8:
            above_ref[:MW] = part[7 * MW :].astype(BF16)
        if start == 16:
            own_ref[TR * MW :] = part[:MW]
            above_ref[MW : 9 * MW] = part.astype(BF16)
        if start == 24:
            above_ref[9 * MW :] = part.astype(BF16)
    put = pltpu.make_async_copy(own_ref, own_hbm, sem)
    put.start()
    first = core_ref[0] == 0
    for a in range(3):
        part = jnp.dot(
            turned_ref[...],
            map_ref[(3 - a) * MW : (3 - a + 2 * TR) * MW],
            preferred_element_type=F32,
        )
        part = part.reshape(3, CHIPS, 2, CIN, C)
        for e in range(3):
            at = (a * 3 + e) * CIN
            keep_ref[:, at : at + CIN, :] = jnp.where(first, part[e, :, 0], part[e, :, 1])
            give_ref[:, at : at + CIN, :] = jnp.where(first, part[e, :, 1], part[e, :, 0]).astype(BF16)
    put.wait()


def filter_part(core, got, features, before, after):
    return pl.pallas_call(
        filter_kernel,
        out_shape=(
            jax.ShapeDtypeStruct((CHIPS, NPART, C), F32),
            jax.ShapeDtypeStruct((CHIPS, NPART, C), BF16),
            pltpu.HBM(((TR + 1) * MW, C), F32),
            jax.ShapeDtypeStruct((REACH * MW, C), BF16),
            jax.ShapeDtypeStruct((MW, C), BF16),
        ),
        in_specs=[pl.BlockSpec(memory_space=pltpu.SMEM), vmem(), vmem(), vmem(), vmem()],
        out_specs=(vmem(), vmem(), hbm(), vmem(), vmem()),
        scratch_shapes=[
            pltpu.VMEM((32, KDIM), F32),
            pltpu.VMEM((MW, KDIM), BF16),
            pltpu.VMEM((8 * MW, KDIM), BF16),
            pltpu.VMEM(((EXT + 6) * MW, C), BF16),
            pltpu.VMEM((3 * C, 2 * TR * MW), BF16),
            pltpu.VMEM(((TR + 1) * MW, C), F32),
            pltpu.SemaphoreType.DMA,
        ],
        compiler_params=pltpu.CompilerParams(vmem_limit_bytes=30 << 20),
        name="filter",
        cost_estimate=cost(2 * EXT * MW * KDIM * C + 36 * TR * MW * C * C, 4 << 20),
    )(core, got, features, before, after)


def input_kernel(own_ref, above_ref, below_ref, weight_ref, out_ref, shifted_ref):
    whole = jnp.concatenate(
        [
            above_ref[:MW].astype(F32),
            own_ref[: (REACH - 1) * MW] + above_ref[MW:].astype(F32),
            own_ref[(REACH - 1) * MW : TR * MW],
            own_ref[TR * MW :] + below_ref[...].astype(F32),
        ],
        axis=0,
    )
    for e, moved in shifts(whole, 2, 0).items():
        shifted_ref[e] = moved
    total = jnp.zeros((TR * MW, C), F32)
    for a in range(3):
        for e in range(3):
            total = total + lax.dot_general(
                shifted_ref[e, (2 - a) * MW : (2 - a + TR) * MW],
                weight_ref[a * 3 + e],
                (((1,), (1,)), ((), ())),
                preferred_element_type=F32,
            )
    out_ref[...] = total.astype(BF16)


def input_part(own, above, below, weight):
    return pl.pallas_call(
        input_kernel,
        out_shape=jax.ShapeDtypeStruct((TR * MW, C), BF16),
        in_specs=[vmem()] * 4,
        out_specs=vmem(),
        scratch_shapes=[pltpu.VMEM((3, (TR + 2) * MW, C), BF16)],
        compiler_params=pltpu.CompilerParams(vmem_limit_bytes=16 << 20),
        name="input",
        cost_estimate=cost(18 * TR * MW * C * C, 4 << 20),
    )(own, above, below, weight)


def sum_kernel(scale, parts_ref, out_ref):
    total = parts_ref[0].astype(F32)
    for i in range(1, parts_ref.shape[0]):
        total = total + parts_ref[i].astype(F32)
    out_ref[...] = jnp.broadcast_to((total * scale).astype(out_ref.dtype), out_ref.shape)


def sum_parts(parts, shape, dtype, scale=1.0):
    return pl.pallas_call(
        functools.partial(sum_kernel, scale),
        out_shape=jax.ShapeDtypeStruct(shape, dtype),
        in_specs=[vmem()],
        out_specs=vmem(),
        compiler_params=pltpu.CompilerParams(vmem_limit_bytes=4 << 20),
        name="sum",
        cost_estimate=cost(parts.size, parts.size * 2),
    )(parts)


PIECES = 4


def pair_kernel(keep_ref, got_ref, out_hbm, out_ref, sems):
    step = CHIPS // PIECES
    sent = []
    for i in range(PIECES):
        part = pl.ds(i * step, step)
        out_ref[part] = (keep_ref[part] + got_ref[part].astype(F32)).astype(BF16)
        sent.append(pltpu.make_async_copy(out_ref.at[part], out_hbm.at[part], sems.at[i]))
        sent[-1].start()
    for copy in sent:
        copy.wait()


def sum_pair(keep, got):
    return pl.pallas_call(
        pair_kernel,
        out_shape=pltpu.HBM(keep.shape, BF16),
        in_specs=[vmem()] * 2,
        out_specs=hbm(),
        scratch_shapes=[pltpu.VMEM(keep.shape, BF16), pltpu.SemaphoreType.DMA((PIECES,))],
        compiler_params=pltpu.CompilerParams(vmem_limit_bytes=4 << 20),
        name="pair",
        cost_estimate=cost(keep.size, keep.size * 8),
    )(keep, got)


def exchange(parts, axis):
    return lax.all_to_all(parts, axis, split_axis=0, concat_axis=0, tiled=True)


def body(features, weight, pool_grad, hard_index, boxes):
    grads = pool_grad[0].transpose(1, 2, 0, 3).reshape(CELLS, ROI_DEV, C)
    send = dispatch(hard_index, boxes[0].T, grads)
    up = [(t, t + 1) for t in range(TILES - 1)]
    down = [(b, a) for a, b in up]
    feature_rows = features[0].reshape(TR * MW, C)
    before = lax.ppermute(feature_rows[(TR - 1) * MW :], TILE_AXES, up)
    after = lax.ppermute(feature_rows[: REACH * MW], TILE_AXES, down)
    got = exchange(send, TILE_AXES)
    core = lax.axis_index("core").reshape(1)
    keep, give, own, above, below = filter_part(core, got, feature_rows, before, after)
    taken = lax.ppermute(give, "core", [(0, 1), (1, 0)])
    parts = exchange(sum_pair(keep, taken), "chip")
    below = lax.ppermute(below, TILE_AXES, down)
    parts, below = lax.optimization_barrier((parts, below))
    parts = exchange(sum_parts(parts, (4, NPART, C), BF16), "zl")
    above = lax.ppermute(above, TILE_AXES, up)
    x_grad = input_part(own, above, below, weight.reshape(9, C, C)).reshape(1, TR, MW, C)
    parts, x_grad = lax.optimization_barrier((parts, x_grad))
    parts = sum_parts(parts, (1, NPART, C), BF16)
    parts = lax.all_gather(parts, "zh", tiled=True, axis_index_groups=[[0, 1], [2, 3]])
    parts = sum_parts(parts, (1, NPART, C), BF16)
    parts = lax.all_gather(parts, "zh", tiled=True, axis_index_groups=[[0, 3], [1, 2]])
    total = sum_parts(parts, (NPART, C), F32, 1.0 / IMAGES)
    total = total.reshape(9, CIN, C).transpose(1, 0, 2).reshape(CIN, 3, 3, C)
    return x_grad, total


def solution(mesh):
    split = Mesh(mesh.devices.reshape(4, 4, CHIPS, 2), ("zh", "zl", "chip", "core"))
    images = ("zh", "zl")
    return jax.shard_map(
        body,
        mesh=split,
        in_specs=(
            P(images, TILE_AXES, None, None),
            P(),
            P(images, TILE_AXES, None, None, None),
            P(images, TILE_AXES),
            P(images, None, None),
        ),
        out_specs=(P(images, TILE_AXES, None, None), P(TILE_AXES, None, None, None)),
        check_vma=False,
    )
```

```python
import functools

import jax
import jax.numpy as jnp
from jax import lax
from jax.experimental import pallas as pl
from jax.experimental.pallas import tpu as pltpu
from jax.sharding import Mesh, PartitionSpec as P

C = 256
TR = 16
MW = 64
ROI_DEV = 16
CAP = 2
REACH = 14
BINS = 7
CELLS = BINS * BINS
PROPS = 20000
TILES = 32
CHIPS = TILES // 2
IMAGES = 16
EXT = TR + REACH - 1
ROWS = 2
SLOT = CELLS + 1
BLOCK = 104
SLOTS = TILES * CAP
KDIM = TILES * BLOCK
LANES = 128
WHOLE = PROPS // LANES * LANES
F32 = jnp.float32
BF16 = jnp.bfloat16
I32 = jnp.int32
CIN = C // TILES
TILE_AXES = ("chip", "core")
NPART = 9 * CIN


def vmem():
    return pl.BlockSpec(memory_space=pltpu.VMEM)


def hbm():
    return pl.BlockSpec(memory_space=pltpu.HBM)


def cost(flops, moved):
    return pl.CostEstimate(flops=flops, bytes_accessed=moved, transcendentals=0)


def iota(shape, dim):
    return lax.broadcasted_iota(I32, shape, dim)


def dispatch_kernel(
    index_hbm, boxes_hbm, grad_hbm, out_hbm, index_ref, boxes_ref, source_ref, sent_ref, sems
):
    copies = [
        pltpu.make_async_copy(index_hbm, index_ref, sems.at[0]),
        pltpu.make_async_copy(boxes_hbm, boxes_ref, sems.at[1]),
        pltpu.make_async_copy(grad_hbm, source_ref.at[:CELLS], sems.at[2]),
    ]
    for copy in copies:
        copy.start()
    copies[0].wait()
    copies[1].wait()
    lane16 = iota((4, ROI_DEV), 1)
    lanes = iota((4, LANES), 1)
    tail = jnp.concatenate(
        [boxes_ref[:, WHOLE:], jnp.zeros((4, LANES - (PROPS - WHOLE)), I32)], axis=1
    )
    chosen = jnp.zeros((4, ROI_DEV), I32)
    for r in range(ROI_DEV):
        index = index_ref[0, r]
        block = index // LANES
        at = jnp.minimum(block, WHOLE // LANES - 1) * LANES
        row = jnp.where(
            block == WHOLE // LANES, tail, boxes_ref[:, pl.ds(pl.multiple_of(at, LANES), LANES)]
        )
        found = jnp.sum(jnp.where(lanes == index - block * LANES, row, 0), axis=1, keepdims=True)
        chosen = jnp.where(lane16 == r, found, chosen)
    chosen = chosen.astype(F32)
    top = chosen[0:1]
    owner = jnp.floor(top * (1.0 / TR))
    local_top = top - owner * TR
    diag = iota((ROI_DEV, ROI_DEV), 0) == iota((ROI_DEV, ROI_DEV), 1)

    def column(row):
        wide = jnp.broadcast_to(row, (ROI_DEV, ROI_DEV))
        return jnp.sum(jnp.where(diag, wide, 0.0), axis=1, keepdims=True)

    before = iota((ROI_DEV, ROI_DEV), 0) < iota((ROI_DEV, ROI_DEV), 1)
    same = column(owner) == owner
    rank = jnp.sum(jnp.where(before & same, 1.0, 0.0), axis=0, keepdims=True)
    field = iota((ROI_DEV, C), 1)
    box_rows = jnp.zeros((ROI_DEV, C), F32)
    for f, row in enumerate((local_top, chosen[1:2], chosen[2:3], chosen[3:4])):
        box_rows = jnp.where(field == f, column(row), box_rows)
    source_ref[CELLS] = box_rows.astype(BF16)
    depth = SLOT * ROI_DEV
    wide = jnp.concatenate([owner, rank, jnp.zeros((6, ROI_DEV), F32)], axis=0).astype(BF16)
    spreading = iota((ROI_DEV, depth), 1) % ROI_DEV == iota((ROI_DEV, depth), 0)
    spread = jnp.dot(wide, spreading.astype(F32).astype(BF16), preferred_element_type=F32)
    cell = (iota((1, depth), 1) // ROI_DEV).astype(F32)
    goal = (spread[0:1] * BLOCK + spread[1:2] * SLOT + cell).astype(I32)
    copies[2].wait()
    source = source_ref[...].reshape(depth, C)
    step = KDIM // 8
    sent = []
    for m in range(8):
        part = pl.ds(m * (TILES // 8), TILES // 8)
        place = iota((step, depth), 0) == goal - m * step
        sent_ref[part] = (
            jnp.dot(place.astype(F32).astype(BF16), source, preferred_element_type=F32)
            .astype(BF16)
            .reshape(TILES // 8, BLOCK, C)
        )
        sent.append(pltpu.make_async_copy(sent_ref.at[part], out_hbm.at[part], sems.at[3 + m]))
        sent[-1].start()
    for copy in sent:
        copy.wait()


def dispatch(index, boxes_t, grads):
    return pl.pallas_call(
        dispatch_kernel,
        out_shape=jax.ShapeDtypeStruct((TILES, BLOCK, C), BF16),
        in_specs=[pl.BlockSpec(memory_space=pl.ANY)] * 3,
        out_specs=pl.BlockSpec(memory_space=pl.ANY),
        scratch_shapes=[
            pltpu.SMEM((1, ROI_DEV), I32),
            pltpu.VMEM((4, PROPS), I32),
            pltpu.VMEM((SLOT, ROI_DEV, C), BF16),
            pltpu.VMEM((TILES, BLOCK, C), BF16),
            pltpu.SemaphoreType.DMA((11,)),
        ],
        compiler_params=pltpu.CompilerParams(vmem_limit_bytes=60 << 20),
        name="dispatch",
        cost_estimate=cost(2 * KDIM * SLOT * ROI_DEV * C, 3 << 20),
    )(*(pltpu.with_memory_space_constraint(x, pltpu.HBM) for x in (index, boxes_t, grads)))


def weights_of(got_ref, rows_ref, cols_ref):
    slot = iota((SLOTS, KDIM), 0)
    cell = iota((SLOTS, KDIM), 1)
    first = (slot % TILES) * BLOCK + (slot // TILES) * SLOT
    box = jnp.concatenate(
        [got_ref[:, s * SLOT + CELLS, :LANES].astype(F32) for s in range(CAP)], axis=0
    )
    box = box.T[:8].astype(BF16)
    cover = ((cell >= first) & (cell < first + CELLS)).astype(F32).astype(BF16)
    field = jnp.dot(box, cover, preferred_element_type=F32).astype(I32)
    within = iota((1, KDIM), 1) % BLOCK
    inside = within < CAP * SLOT
    within = within % SLOT
    inside = inside & (within < CELLS)
    row_bin = within // BINS
    col_bin = within - row_bin * BINS
    row = jnp.where(inside, field[0:1] + row_bin * field[2:3], -9)
    col = field[1:2] + col_bin * field[3:4]
    grid = iota((32, KDIM), 0)
    rows_ref[...] = jnp.where(grid == row, 0.75, jnp.where(grid == row + 1, 0.25, 0.0))
    grid = iota((MW, KDIM), 0)
    cols_ref[...] = jnp.where(grid == col, 0.25, jnp.where(grid == col + 1, 0.75, 0.0)).astype(BF16)


def rows_of(start, count, got_ref, rows_ref, cols_ref, left_ref):
    cols = cols_ref[...]
    for h in range(count):
        left_ref[h * MW : (h + 1) * MW] = cols * rows_ref[start + h : start + h + 1, :].astype(BF16)
    return jnp.dot(
        left_ref[: count * MW], got_ref[...].reshape(KDIM, C), preferred_element_type=F32
    )


def shifts(rows, before, after):
    count = rows.shape[0]
    column = iota((count, C), 0) % MW
    one_less = jnp.where(column == 0, 0.0, pltpu.roll(rows, 1, 0)).astype(BF16)
    one_more = jnp.where(column == MW - 1, 0.0, pltpu.roll(rows, count - 1, 0)).astype(BF16)
    return {before: one_less, 1: rows.astype(BF16), after: one_more}


def turn_rows(rows, out_ref):
    for e, moved in shifts(rows.astype(F32), 0, 2).items():
        out_ref[e * C : (e + 1) * C] = moved.T


def filter_kernel(
    got_ref, features_ref,
    part_ref, beyond_ref, own_hbm, above_ref, below_ref,
    rows_ref, cols_ref, left_ref, map_ref, turned_ref, own_ref, sem,
):
    weights_of(got_ref, rows_ref, cols_ref)
    turn_rows(features_ref[...], turned_ref)
    map_ref[: 2 * MW] = jnp.zeros((2 * MW, C), BF16)
    map_ref[(2 + EXT) * MW :] = jnp.zeros((4 * MW, C), BF16)
    for start in range(0, EXT, ROWS):
        count = min(ROWS, EXT - start)
        part = rows_of(start, count, got_ref, rows_ref, cols_ref, left_ref)
        rounded = part.astype(BF16)
        map_ref[(2 + start) * MW : (2 + start + count) * MW] = rounded
        for h in range(start, start + count):
            one = slice((h - start) * MW, (h - start + 1) * MW)
            if h <= TR:
                own_ref[h * MW : (h + 1) * MW] = part[one]
            if h == 0:
                below_ref[...] = rounded[one]
                map_ref[(4 + EXT) * MW : (5 + EXT) * MW] = rounded[one]
            if h >= TR - 1:
                above_ref[(h - TR + 1) * MW : (h - TR + 2) * MW] = rounded[one]
    put = pltpu.make_async_copy(own_ref, own_hbm, sem)
    put.start()
    beyond_ref[...] = map_ref[(1 + TR) * MW : (3 + 2 * TR) * MW]
    for a in range(3):
        part_ref[a] = jnp.dot(
            turned_ref[...],
            map_ref[(3 - a) * MW : (3 - a + TR) * MW],
            preferred_element_type=F32,
        )
    put.wait()


def beyond_kernel(
    core_ref, part_ref, beyond_ref, before_ref, after_ref, keep_ref, give_ref, turned_ref
):
    rows = jnp.concatenate([after_ref[...], before_ref[...], jnp.zeros((MW, C), BF16)], axis=0)
    turn_rows(rows, turned_ref)
    first = core_ref[0] == 0
    for a in range(3):
        part = part_ref[a] + jnp.dot(
            turned_ref[...],
            beyond_ref[(2 - a) * MW : (2 - a + TR) * MW],
            preferred_element_type=F32,
        )
        part = part.reshape(3, CHIPS, 2, CIN, C)
        for e in range(3):
            at = (a * 3 + e) * CIN
            keep_ref[:, at : at + CIN, :] = jnp.where(first, part[e, :, 0], part[e, :, 1])
            give_ref[:, at : at + CIN, :] = jnp.where(first, part[e, :, 1], part[e, :, 0]).astype(BF16)


def beyond_part(core, part, beyond, before, after):
    return pl.pallas_call(
        beyond_kernel,
        out_shape=(
            jax.ShapeDtypeStruct((CHIPS, NPART, C), F32),
            jax.ShapeDtypeStruct((CHIPS, NPART, C), BF16),
        ),
        in_specs=[pl.BlockSpec(memory_space=pltpu.SMEM)] + [vmem()] * 4,
        out_specs=(vmem(), vmem()),
        scratch_shapes=[pltpu.VMEM((3 * C, TR * MW), BF16)],
        compiler_params=pltpu.CompilerParams(vmem_limit_bytes=16 << 20),
        name="beyond",
        cost_estimate=cost(18 * TR * MW * C * C, 4 << 20),
    )(core, part, beyond, before, after)


def filter_part(got, features):
    return pl.pallas_call(
        filter_kernel,
        out_shape=(
            jax.ShapeDtypeStruct((3, 3 * C, C), F32),
            jax.ShapeDtypeStruct(((TR + 2) * MW, C), BF16),
            pltpu.HBM(((TR + 1) * MW, C), F32),
            jax.ShapeDtypeStruct((REACH * MW, C), BF16),
            jax.ShapeDtypeStruct((MW, C), BF16),
        ),
        in_specs=[vmem(), vmem()],
        out_specs=(vmem(), vmem(), hbm(), vmem(), vmem()),
        scratch_shapes=[
            pltpu.VMEM((32, KDIM), F32),
            pltpu.VMEM((MW, KDIM), BF16),
            pltpu.VMEM((ROWS * MW, KDIM), BF16),
            pltpu.VMEM(((EXT + 6) * MW, C), BF16),
            pltpu.VMEM((3 * C, TR * MW), BF16),
            pltpu.VMEM(((TR + 1) * MW, C), F32),
            pltpu.SemaphoreType.DMA,
        ],
        compiler_params=pltpu.CompilerParams(vmem_limit_bytes=30 << 20),
        name="filter",
        cost_estimate=cost(2 * EXT * MW * KDIM * C + 36 * TR * MW * C * C, 4 << 20),
    )(got, features)


def input_kernel(own_ref, above_ref, below_ref, weight_ref, out_ref, shifted_ref):
    whole = jnp.concatenate(
        [
            above_ref[:MW].astype(F32),
            own_ref[: (REACH - 1) * MW] + above_ref[MW:].astype(F32),
            own_ref[(REACH - 1) * MW : TR * MW],
            own_ref[TR * MW :] + below_ref[...].astype(F32),
        ],
        axis=0,
    )
    for e, moved in shifts(whole, 2, 0).items():
        shifted_ref[e] = moved
    total = jnp.zeros((TR * MW, C), F32)
    for a in range(3):
        for e in range(3):
            total = total + lax.dot_general(
                shifted_ref[e, (2 - a) * MW : (2 - a + TR) * MW],
                weight_ref[a * 3 + e],
                (((1,), (1,)), ((), ())),
                preferred_element_type=F32,
            )
    out_ref[...] = total.astype(BF16)


def input_part(own, above, below, weight):
    return pl.pallas_call(
        input_kernel,
        out_shape=jax.ShapeDtypeStruct((TR * MW, C), BF16),
        in_specs=[vmem()] * 4,
        out_specs=vmem(),
        scratch_shapes=[pltpu.VMEM((3, (TR + 2) * MW, C), BF16)],
        compiler_params=pltpu.CompilerParams(vmem_limit_bytes=16 << 20),
        name="input",
        cost_estimate=cost(18 * TR * MW * C * C, 4 << 20),
    )(own, above, below, weight)


def sum_kernel(scale, parts_ref, out_ref):
    total = parts_ref[0].astype(F32)
    for i in range(1, parts_ref.shape[0]):
        total = total + parts_ref[i].astype(F32)
    out_ref[...] = jnp.broadcast_to((total * scale).astype(out_ref.dtype), out_ref.shape)


def sum_parts(parts, shape, dtype, scale=1.0):
    return pl.pallas_call(
        functools.partial(sum_kernel, scale),
        out_shape=jax.ShapeDtypeStruct(shape, dtype),
        in_specs=[vmem()],
        out_specs=vmem(),
        compiler_params=pltpu.CompilerParams(vmem_limit_bytes=4 << 20),
        name="sum",
        cost_estimate=cost(parts.size, parts.size * 2),
    )(parts)


PIECES = 4


def pair_kernel(keep_ref, got_ref, out_hbm, out_ref, sems):
    step = CHIPS // PIECES
    sent = []
    for i in range(PIECES):
        part = pl.ds(i * step, step)
        out_ref[part] = (keep_ref[part] + got_ref[part].astype(F32)).astype(BF16)
        sent.append(pltpu.make_async_copy(out_ref.at[part], out_hbm.at[part], sems.at[i]))
        sent[-1].start()
    for copy in sent:
        copy.wait()


def sum_pair(keep, got):
    return pl.pallas_call(
        pair_kernel,
        out_shape=pltpu.HBM(keep.shape, BF16),
        in_specs=[vmem()] * 2,
        out_specs=hbm(),
        scratch_shapes=[pltpu.VMEM(keep.shape, BF16), pltpu.SemaphoreType.DMA((PIECES,))],
        compiler_params=pltpu.CompilerParams(vmem_limit_bytes=4 << 20),
        name="pair",
        cost_estimate=cost(keep.size, keep.size * 8),
    )(keep, got)


def exchange(parts, axis):
    return lax.all_to_all(parts, axis, split_axis=0, concat_axis=0, tiled=True)


def body(features, weight, pool_grad, hard_index, boxes):
    grads = pool_grad[0].transpose(1, 2, 0, 3).reshape(CELLS, ROI_DEV, C)
    send = dispatch(hard_index, boxes[0].T, grads)
    up = [(t, t + 1) for t in range(TILES - 1)]
    down = [(b, a) for a, b in up]
    feature_rows = features[0].reshape(TR * MW, C)
    before = lax.ppermute(feature_rows[(TR - 1) * MW :], TILE_AXES, up)
    after = lax.ppermute(feature_rows[: REACH * MW], TILE_AXES, down)
    got = exchange(send, TILE_AXES)
    core = lax.axis_index("core").reshape(1)
    part, beyond, own, above, below = filter_part(got, feature_rows)
    keep, give = beyond_part(core, part, beyond, before, after)
    taken = lax.ppermute(give, "core", [(0, 1), (1, 0)])
    parts = exchange(sum_pair(keep, taken), "chip")
    below = lax.ppermute(below, TILE_AXES, down)
    parts, below = lax.optimization_barrier((parts, below))
    parts = exchange(sum_parts(parts, (4, NPART, C), BF16), "zl")
    above = lax.ppermute(above, TILE_AXES, up)
    x_grad = input_part(own, above, below, weight.reshape(9, C, C)).reshape(1, TR, MW, C)
    parts, x_grad = lax.optimization_barrier((parts, x_grad))
    parts = sum_parts(parts, (1, NPART, C), BF16)
    parts = lax.all_gather(parts, "zh", tiled=True, axis_index_groups=[[0, 1], [2, 3]])
    parts = sum_parts(parts, (1, NPART, C), BF16)
    parts = lax.all_gather(parts, "zh", tiled=True, axis_index_groups=[[0, 3], [1, 2]])
    total = sum_parts(parts, (NPART, C), F32, 1.0 / IMAGES)
    total = total.reshape(9, CIN, C).transpose(1, 0, 2).reshape(CIN, 3, 3, C)
    return x_grad, total


def solution(mesh):
    split = Mesh(mesh.devices.reshape(4, 4, CHIPS, 2), ("zh", "zl", "chip", "core"))
    images = ("zh", "zl")
    return jax.shard_map(
        body,
        mesh=split,
        in_specs=(
            P(images, TILE_AXES, None, None),
            P(),
            P(images, TILE_AXES, None, None, None),
            P(images, TILE_AXES),
            P(images, None, None),
        ),
        out_specs=(P(images, TILE_AXES, None, None), P(TILE_AXES, None, None, None)),
        check_vma=False,
    )
```

```python
import functools

import jax
import jax.numpy as jnp
from jax import lax
from jax.experimental import pallas as pl
from jax.experimental.pallas import tpu as pltpu
from jax.sharding import Mesh, PartitionSpec as P

C = 256
TR = 16
MW = 64
ROI_DEV = 16
CAP = 2
REACH = 14
BINS = 7
CELLS = BINS * BINS
PROPS = 20000
TILES = 32
CHIPS = TILES // 2
IMAGES = 16
EXT = TR + REACH - 1
ROWS = 3
SLOT = CELLS + 1
BLOCK = 104
SLOTS = TILES * CAP
KDIM = TILES * BLOCK
LANES = 128
WHOLE = PROPS // LANES * LANES
F32 = jnp.float32
BF16 = jnp.bfloat16
I32 = jnp.int32
CIN = C // TILES
TILE_AXES = ("chip", "core")
NPART = 9 * CIN


def vmem():
    return pl.BlockSpec(memory_space=pltpu.VMEM)


def cost(flops, moved):
    return pl.CostEstimate(flops=flops, bytes_accessed=moved, transcendentals=0)


def iota(shape, dim):
    return lax.broadcasted_iota(I32, shape, dim)


def dispatch_kernel(index_ref, boxes_ref, grad_ref, out_ref):
    lane16 = iota((4, ROI_DEV), 1)
    lanes = iota((4, LANES), 1)
    tail = jnp.concatenate(
        [boxes_ref[:, WHOLE:], jnp.zeros((4, LANES - (PROPS - WHOLE)), I32)], axis=1
    )
    chosen = jnp.zeros((4, ROI_DEV), I32)
    for r in range(ROI_DEV):
        index = index_ref[0, r]
        block = index // LANES
        at = jnp.minimum(block, WHOLE // LANES - 1) * LANES
        row = jnp.where(
            block == WHOLE // LANES, tail, boxes_ref[:, pl.ds(pl.multiple_of(at, LANES), LANES)]
        )
        found = jnp.sum(jnp.where(lanes == index - block * LANES, row, 0), axis=1, keepdims=True)
        chosen = jnp.where(lane16 == r, found, chosen)
    chosen = chosen.astype(F32)
    top = chosen[0:1]
    owner = jnp.floor(top * (1.0 / TR))
    local_top = top - owner * TR
    diag = iota((ROI_DEV, ROI_DEV), 0) == iota((ROI_DEV, ROI_DEV), 1)

    def column(row):
        wide = jnp.broadcast_to(row, (ROI_DEV, ROI_DEV))
        return jnp.sum(jnp.where(diag, wide, 0.0), axis=1, keepdims=True)

    before = iota((ROI_DEV, ROI_DEV), 0) < iota((ROI_DEV, ROI_DEV), 1)
    same = column(owner) == owner
    rank = jnp.sum(jnp.where(before & same, 1.0, 0.0), axis=0, keepdims=True)
    field = iota((ROI_DEV, C), 1)
    box_rows = jnp.zeros((ROI_DEV, C), F32)
    for f, row in enumerate((local_top, chosen[1:2], chosen[2:3], chosen[3:4])):
        box_rows = jnp.where(field == f, column(row), box_rows)
    depth = SLOT * ROI_DEV
    wide = jnp.concatenate([owner, rank, jnp.zeros((6, ROI_DEV), F32)], axis=0).astype(BF16)
    spreading = iota((ROI_DEV, depth), 1) % ROI_DEV == iota((ROI_DEV, depth), 0)
    spread = jnp.dot(wide, spreading.astype(F32).astype(BF16), preferred_element_type=F32)
    cell = (iota((1, depth), 1) // ROI_DEV).astype(F32)
    goal = (spread[0:1] * BLOCK + spread[1:2] * SLOT + cell).astype(I32)
    source = jnp.concatenate(
        [grad_ref[...].reshape(CELLS * ROI_DEV, C), box_rows.astype(BF16)], axis=0
    )
    step = KDIM // 8
    for m in range(8):
        place = iota((step, depth), 0) == goal - m * step
        out_ref[m * (TILES // 8) : (m + 1) * (TILES // 8)] = (
            jnp.dot(place.astype(F32).astype(BF16), source, preferred_element_type=F32)
            .astype(BF16)
            .reshape(TILES // 8, BLOCK, C)
        )


def dispatch(index, boxes_t, grads):
    return pl.pallas_call(
        dispatch_kernel,
        out_shape=jax.ShapeDtypeStruct((TILES, BLOCK, C), BF16),
        in_specs=[pl.BlockSpec(memory_space=pltpu.SMEM), vmem(), vmem()],
        out_specs=vmem(),
        compiler_params=pltpu.CompilerParams(vmem_limit_bytes=60 << 20),
        name="dispatch",
        cost_estimate=cost(2 * KDIM * SLOT * ROI_DEV * C, 3 << 20),
    )(index, boxes_t, grads)


def weights_of(got_ref, rows_ref, cols_ref):
    slot = iota((SLOTS, KDIM), 0)
    cell = iota((SLOTS, KDIM), 1)
    first = (slot % TILES) * BLOCK + (slot // TILES) * SLOT
    box = jnp.concatenate(
        [got_ref[:, s * SLOT + CELLS, :LANES].astype(F32) for s in range(CAP)], axis=0
    )
    box = box.T[:8].astype(BF16)
    cover = ((cell >= first) & (cell < first + CELLS)).astype(F32).astype(BF16)
    field = jnp.dot(box, cover, preferred_element_type=F32).astype(I32)
    within = iota((1, KDIM), 1) % BLOCK
    inside = within < CAP * SLOT
    within = within % SLOT
    inside = inside & (within < CELLS)
    row_bin = within // BINS
    col_bin = within - row_bin * BINS
    row = jnp.where(inside, field[0:1] + row_bin * field[2:3], -9)
    col = field[1:2] + col_bin * field[3:4]
    grid = iota((32, KDIM), 0)
    rows_ref[...] = jnp.where(grid == row, 0.75, jnp.where(grid == row + 1, 0.25, 0.0))
    grid = iota((MW, KDIM), 0)
    cols_ref[...] = jnp.where(grid == col, 0.25, jnp.where(grid == col + 1, 0.75, 0.0)).astype(BF16)


def rows_of(start, count, got_ref, rows_ref, cols_ref, left_ref):
    cols = cols_ref[...]
    for h in range(count):
        left_ref[h * MW : (h + 1) * MW] = cols * rows_ref[start + h : start + h + 1, :].astype(BF16)
    return jnp.dot(
        left_ref[: count * MW], got_ref[...].reshape(KDIM, C), preferred_element_type=F32
    )


def shifts(rows, before, after):
    count = rows.shape[0]
    column = iota((count, C), 0) % MW
    one_less = jnp.where(column == 0, 0.0, pltpu.roll(rows, 1, 0)).astype(BF16)
    one_more = jnp.where(column == MW - 1, 0.0, pltpu.roll(rows, count - 1, 0)).astype(BF16)
    return {before: one_less, 1: rows.astype(BF16), after: one_more}


def turn_rows(rows, out_ref):
    for e, moved in shifts(rows.astype(F32), 0, 2).items():
        out_ref[e * C : (e + 1) * C] = moved.T


def filter_kernel(
    got_ref, features_ref,
    part_ref, beyond_ref, own_ref, above_ref, below_ref,
    rows_ref, cols_ref, left_ref, map_ref, turned_ref,
):
    weights_of(got_ref, rows_ref, cols_ref)
    turn_rows(features_ref[...], turned_ref)
    map_ref[: 2 * MW] = jnp.zeros((2 * MW, C), BF16)
    map_ref[(2 + EXT) * MW :] = jnp.zeros((4 * MW, C), BF16)
    for start in range(0, EXT, ROWS):
        count = min(ROWS, EXT - start)
        part = rows_of(start, count, got_ref, rows_ref, cols_ref, left_ref)
        rounded = part.astype(BF16)
        map_ref[(2 + start) * MW : (2 + start + count) * MW] = rounded
        for h in range(start, start + count):
            one = slice((h - start) * MW, (h - start + 1) * MW)
            if h <= TR:
                own_ref[h * MW : (h + 1) * MW] = part[one]
            if h == 0:
                below_ref[...] = rounded[one]
                map_ref[(4 + EXT) * MW : (5 + EXT) * MW] = rounded[one]
            if h >= TR - 1:
                above_ref[(h - TR + 1) * MW : (h - TR + 2) * MW] = rounded[one]
    beyond_ref[...] = map_ref[(1 + TR) * MW : (3 + 2 * TR) * MW]
    for a in range(3):
        part_ref[a] = jnp.dot(
            turned_ref[...],
            map_ref[(3 - a) * MW : (3 - a + TR) * MW],
            preferred_element_type=F32,
        )


def beyond_kernel(
    core_ref, part_ref, beyond_ref, before_ref, after_ref, keep_ref, give_ref, turned_ref
):
    rows = jnp.concatenate([after_ref[...], before_ref[...], jnp.zeros((MW, C), BF16)], axis=0)
    turn_rows(rows, turned_ref)
    first = core_ref[0] == 0
    for a in range(3):
        part = part_ref[a] + jnp.dot(
            turned_ref[...],
            beyond_ref[(2 - a) * MW : (2 - a + TR) * MW],
            preferred_element_type=F32,
        )
        part = part.reshape(3, CHIPS, 2, CIN, C)
        for e in range(3):
            at = (a * 3 + e) * CIN
            keep_ref[:, at : at + CIN, :] = jnp.where(first, part[e, :, 0], part[e, :, 1])
            give_ref[:, at : at + CIN, :] = jnp.where(first, part[e, :, 1], part[e, :, 0]).astype(BF16)


def beyond_part(core, part, beyond, before, after):
    return pl.pallas_call(
        beyond_kernel,
        out_shape=(
            jax.ShapeDtypeStruct((CHIPS, NPART, C), F32),
            jax.ShapeDtypeStruct((CHIPS, NPART, C), BF16),
        ),
        in_specs=[pl.BlockSpec(memory_space=pltpu.SMEM)] + [vmem()] * 4,
        out_specs=(vmem(), vmem()),
        scratch_shapes=[pltpu.VMEM((3 * C, TR * MW), BF16)],
        compiler_params=pltpu.CompilerParams(vmem_limit_bytes=16 << 20),
        name="beyond",
        cost_estimate=cost(18 * TR * MW * C * C, 4 << 20),
    )(core, part, beyond, before, after)


def filter_part(got, features):
    return pl.pallas_call(
        filter_kernel,
        out_shape=(
            jax.ShapeDtypeStruct((3, 3 * C, C), F32),
            jax.ShapeDtypeStruct(((TR + 2) * MW, C), BF16),
            jax.ShapeDtypeStruct(((TR + 1) * MW, C), F32),
            jax.ShapeDtypeStruct((REACH * MW, C), BF16),
            jax.ShapeDtypeStruct((MW, C), BF16),
        ),
        in_specs=[vmem(), vmem()],
        out_specs=(vmem(),) * 5,
        scratch_shapes=[
            pltpu.VMEM((32, KDIM), F32),
            pltpu.VMEM((MW, KDIM), BF16),
            pltpu.VMEM((ROWS * MW, KDIM), BF16),
            pltpu.VMEM(((EXT + 6) * MW, C), BF16),
            pltpu.VMEM((3 * C, TR * MW), BF16),
        ],
        compiler_params=pltpu.CompilerParams(vmem_limit_bytes=30 << 20),
        name="filter",
        cost_estimate=cost(2 * EXT * MW * KDIM * C + 36 * TR * MW * C * C, 4 << 20),
    )(got, features)


def input_kernel(own_ref, above_ref, below_ref, weight_ref, out_ref, shifted_ref):
    whole = jnp.concatenate(
        [
            above_ref[:MW].astype(F32),
            own_ref[: (REACH - 1) * MW] + above_ref[MW:].astype(F32),
            own_ref[(REACH - 1) * MW : TR * MW],
            own_ref[TR * MW :] + below_ref[...].astype(F32),
        ],
        axis=0,
    )
    for e, moved in shifts(whole, 2, 0).items():
        shifted_ref[e] = moved
    total = jnp.zeros((TR * MW, C), F32)
    for a in range(3):
        for e in range(3):
            total = total + lax.dot_general(
                shifted_ref[e, (2 - a) * MW : (2 - a + TR) * MW],
                weight_ref[a * 3 + e],
                (((1,), (1,)), ((), ())),
                preferred_element_type=F32,
            )
    out_ref[...] = total.astype(BF16)


def input_part(own, above, below, weight):
    return pl.pallas_call(
        input_kernel,
        out_shape=jax.ShapeDtypeStruct((TR * MW, C), BF16),
        in_specs=[vmem()] * 4,
        out_specs=vmem(),
        scratch_shapes=[pltpu.VMEM((3, (TR + 2) * MW, C), BF16)],
        compiler_params=pltpu.CompilerParams(vmem_limit_bytes=16 << 20),
        name="input",
        cost_estimate=cost(18 * TR * MW * C * C, 4 << 20),
    )(own, above, below, weight)


def sum_kernel(scale, parts_ref, out_ref):
    total = parts_ref[0].astype(F32)
    for i in range(1, parts_ref.shape[0]):
        total = total + parts_ref[i].astype(F32)
    out_ref[...] = jnp.broadcast_to((total * scale).astype(out_ref.dtype), out_ref.shape)


def sum_parts(parts, shape, dtype, scale=1.0):
    return pl.pallas_call(
        functools.partial(sum_kernel, scale),
        out_shape=jax.ShapeDtypeStruct(shape, dtype),
        in_specs=[vmem()],
        out_specs=vmem(),
        compiler_params=pltpu.CompilerParams(vmem_limit_bytes=4 << 20),
        name="sum",
        cost_estimate=cost(parts.size, parts.size * 2),
    )(parts)


def pair_kernel(keep_ref, got_ref, out_ref):
    out_ref[...] = (keep_ref[...] + got_ref[...].astype(F32)).astype(BF16)


def sum_pair(keep, got):
    return pl.pallas_call(
        pair_kernel,
        out_shape=jax.ShapeDtypeStruct(keep.shape, BF16),
        in_specs=[vmem()] * 2,
        out_specs=vmem(),
        compiler_params=pltpu.CompilerParams(vmem_limit_bytes=4 << 20),
        name="pair",
        cost_estimate=cost(keep.size, keep.size * 8),
    )(keep, got)


def exchange(parts, axis):
    return lax.all_to_all(parts, axis, split_axis=0, concat_axis=0, tiled=True)


def body(features, weight, pool_grad, hard_index, boxes):
    grads = pool_grad[0].transpose(1, 2, 0, 3).reshape(CELLS, ROI_DEV, C)
    send = dispatch(hard_index, boxes[0].T, grads)
    up = [(t, t + 1) for t in range(TILES - 1)]
    down = [(b, a) for a, b in up]
    feature_rows = features[0].reshape(TR * MW, C)
    before = lax.ppermute(feature_rows[(TR - 1) * MW :], TILE_AXES, up)
    after = lax.ppermute(feature_rows[: REACH * MW], TILE_AXES, down)
    got = exchange(send, TILE_AXES)
    core = lax.axis_index("core").reshape(1)
    part, beyond, own, above, below = filter_part(got, feature_rows)
    keep, give = beyond_part(core, part, beyond, before, after)
    taken = lax.ppermute(give, "core", [(0, 1), (1, 0)])
    parts = exchange(sum_pair(keep, taken), "chip")
    below = lax.ppermute(below, TILE_AXES, down)
    parts, below = lax.optimization_barrier((parts, below))
    parts = exchange(sum_parts(parts, (4, NPART, C), BF16), "zl")
    above = lax.ppermute(above, TILE_AXES, up)
    x_grad = input_part(own, above, below, weight.reshape(9, C, C)).reshape(1, TR, MW, C)
    parts, x_grad = lax.optimization_barrier((parts, x_grad))
    parts = sum_parts(parts, (1, NPART, C), BF16)
    parts = lax.all_gather(parts, "zh", tiled=True, axis_index_groups=[[0, 1], [2, 3]])
    parts = sum_parts(parts, (1, NPART, C), BF16)
    parts = lax.all_gather(parts, "zh", tiled=True, axis_index_groups=[[0, 3], [1, 2]])
    total = sum_parts(parts, (NPART, C), F32, 1.0 / IMAGES)
    total = total.reshape(9, CIN, C).transpose(1, 0, 2).reshape(CIN, 3, 3, C)
    return x_grad, total


def solution(mesh):
    split = Mesh(mesh.devices.reshape(4, 4, CHIPS, 2), ("zh", "zl", "chip", "core"))
    images = ("zh", "zl")
    return jax.shard_map(
        body,
        mesh=split,
        in_specs=(
            P(images, TILE_AXES, None, None),
            P(),
            P(images, TILE_AXES, None, None, None),
            P(images, TILE_AXES),
            P(images, None, None),
        ),
        out_specs=(P(images, TILE_AXES, None, None), P(TILE_AXES, None, None, None)),
        check_vma=False,
    )
```

```python
import functools

import jax
import jax.numpy as jnp
from jax import lax
from jax.experimental import pallas as pl
from jax.experimental.pallas import tpu as pltpu
from jax.sharding import Mesh, PartitionSpec as P

C = 256
TR = 16
MW = 64
ROI_DEV = 16
CAP = 2
REACH = 14
BINS = 7
CELLS = BINS * BINS
PROPS = 20000
TILES = 32
CHIPS = TILES // 2
IMAGES = 16
EXT = TR + REACH - 1
ROWS = 3
SLOT = CELLS + 1
BLOCK = 104
SLOTS = TILES * CAP
KDIM = TILES * BLOCK
LANES = 128
WHOLE = PROPS // LANES * LANES
F32 = jnp.float32
BF16 = jnp.bfloat16
I32 = jnp.int32
CIN = C // TILES
TILE_AXES = ("chip", "core")
NPART = 9 * CIN


def vmem():
    return pl.BlockSpec(memory_space=pltpu.VMEM)


def hbm():
    return pl.BlockSpec(memory_space=pltpu.HBM)


def cost(flops, moved):
    return pl.CostEstimate(flops=flops, bytes_accessed=moved, transcendentals=0)


def iota(shape, dim):
    return lax.broadcasted_iota(I32, shape, dim)


def dispatch_kernel(
    index_hbm, boxes_hbm, grad_hbm, out_hbm, index_ref, boxes_ref, source_ref, sent_ref, sems
):
    copies = [
        pltpu.make_async_copy(index_hbm, index_ref, sems.at[0]),
        pltpu.make_async_copy(boxes_hbm, boxes_ref, sems.at[1]),
        pltpu.make_async_copy(grad_hbm, source_ref.at[:CELLS], sems.at[2]),
    ]
    for copy in copies:
        copy.start()
    copies[0].wait()
    copies[1].wait()
    lane16 = iota((4, ROI_DEV), 1)
    lanes = iota((4, LANES), 1)
    tail = jnp.concatenate(
        [boxes_ref[:, WHOLE:], jnp.zeros((4, LANES - (PROPS - WHOLE)), I32)], axis=1
    )
    chosen = jnp.zeros((4, ROI_DEV), I32)
    for r in range(ROI_DEV):
        index = index_ref[0, r]
        block = index // LANES
        at = jnp.minimum(block, WHOLE // LANES - 1) * LANES
        row = jnp.where(
            block == WHOLE // LANES, tail, boxes_ref[:, pl.ds(pl.multiple_of(at, LANES), LANES)]
        )
        found = jnp.sum(jnp.where(lanes == index - block * LANES, row, 0), axis=1, keepdims=True)
        chosen = jnp.where(lane16 == r, found, chosen)
    chosen = chosen.astype(F32)
    top = chosen[0:1]
    owner = jnp.floor(top * (1.0 / TR))
    local_top = top - owner * TR
    diag = iota((ROI_DEV, ROI_DEV), 0) == iota((ROI_DEV, ROI_DEV), 1)

    def column(row):
        wide = jnp.broadcast_to(row, (ROI_DEV, ROI_DEV))
        return jnp.sum(jnp.where(diag, wide, 0.0), axis=1, keepdims=True)

    before = iota((ROI_DEV, ROI_DEV), 0) < iota((ROI_DEV, ROI_DEV), 1)
    same = column(owner) == owner
    rank = jnp.sum(jnp.where(before & same, 1.0, 0.0), axis=0, keepdims=True)
    field = iota((ROI_DEV, C), 1)
    box_rows = jnp.zeros((ROI_DEV, C), F32)
    for f, row in enumerate((local_top, chosen[1:2], chosen[2:3], chosen[3:4])):
        box_rows = jnp.where(field == f, column(row), box_rows)
    source_ref[CELLS] = box_rows.astype(BF16)
    depth = SLOT * ROI_DEV
    wide = jnp.concatenate([owner, rank, jnp.zeros((6, ROI_DEV), F32)], axis=0).astype(BF16)
    spreading = iota((ROI_DEV, depth), 1) % ROI_DEV == iota((ROI_DEV, depth), 0)
    spread = jnp.dot(wide, spreading.astype(F32).astype(BF16), preferred_element_type=F32)
    cell = (iota((1, depth), 1) // ROI_DEV).astype(F32)
    goal = (spread[0:1] * BLOCK + spread[1:2] * SLOT + cell).astype(I32)
    copies[2].wait()
    source = source_ref[...].reshape(depth, C)
    step = KDIM // 8
    sent = []
    for m in range(8):
        part = pl.ds(m * (TILES // 8), TILES // 8)
        place = iota((step, depth), 0) == goal - m * step
        sent_ref[part] = (
            jnp.dot(place.astype(F32).astype(BF16), source, preferred_element_type=F32)
            .astype(BF16)
            .reshape(TILES // 8, BLOCK, C)
        )
        sent.append(pltpu.make_async_copy(sent_ref.at[part], out_hbm.at[part], sems.at[3 + m]))
        sent[-1].start()
    for copy in sent:
        copy.wait()


def dispatch(index, boxes_t, grads):
    return pl.pallas_call(
        dispatch_kernel,
        out_shape=jax.ShapeDtypeStruct((TILES, BLOCK, C), BF16),
        in_specs=[pl.BlockSpec(memory_space=pl.ANY)] * 3,
        out_specs=pl.BlockSpec(memory_space=pl.ANY),
        scratch_shapes=[
            pltpu.SMEM((1, ROI_DEV), I32),
            pltpu.VMEM((4, PROPS), I32),
            pltpu.VMEM((SLOT, ROI_DEV, C), BF16),
            pltpu.VMEM((TILES, BLOCK, C), BF16),
            pltpu.SemaphoreType.DMA((11,)),
        ],
        compiler_params=pltpu.CompilerParams(vmem_limit_bytes=60 << 20),
        name="dispatch",
        cost_estimate=cost(2 * KDIM * SLOT * ROI_DEV * C, 3 << 20),
    )(*(pltpu.with_memory_space_constraint(x, pltpu.HBM) for x in (index, boxes_t, grads)))


def weights_of(got_ref, rows_ref, cols_ref):
    slot = iota((SLOTS, KDIM), 0)
    cell = iota((SLOTS, KDIM), 1)
    first = (slot % TILES) * BLOCK + (slot // TILES) * SLOT
    box = jnp.concatenate(
        [got_ref[:, s * SLOT + CELLS, :LANES].astype(F32) for s in range(CAP)], axis=0
    )
    box = box.T[:8].astype(BF16)
    cover = ((cell >= first) & (cell < first + CELLS)).astype(F32).astype(BF16)
    field = jnp.dot(box, cover, preferred_element_type=F32).astype(I32)
    within = iota((1, KDIM), 1) % BLOCK
    inside = within < CAP * SLOT
    within = within % SLOT
    inside = inside & (within < CELLS)
    row_bin = within // BINS
    col_bin = within - row_bin * BINS
    row = jnp.where(inside, field[0:1] + row_bin * field[2:3], -9)
    col = field[1:2] + col_bin * field[3:4]
    grid = iota((32, KDIM), 0)
    rows_ref[...] = jnp.where(grid == row, 0.75, jnp.where(grid == row + 1, 0.25, 0.0))
    grid = iota((MW, KDIM), 0)
    cols_ref[...] = jnp.where(grid == col, 0.25, jnp.where(grid == col + 1, 0.75, 0.0)).astype(BF16)


def rows_of(start, count, got_ref, rows_ref, cols_ref, left_ref):
    cols = cols_ref[...]
    for h in range(count):
        left_ref[h * MW : (h + 1) * MW] = cols * rows_ref[start + h : start + h + 1, :].astype(BF16)
    return jnp.dot(
        left_ref[: count * MW], got_ref[...].reshape(KDIM, C), preferred_element_type=F32
    )


def shifts(rows, before, after):
    count = rows.shape[0]
    column = iota((count, C), 0) % MW
    one_less = jnp.where(column == 0, 0.0, pltpu.roll(rows, 1, 0)).astype(BF16)
    one_more = jnp.where(column == MW - 1, 0.0, pltpu.roll(rows, count - 1, 0)).astype(BF16)
    return {before: one_less, 1: rows.astype(BF16), after: one_more}


def turn_rows(rows, out_ref):
    for e, moved in shifts(rows.astype(F32), 0, 2).items():
        out_ref[e * C : (e + 1) * C] = moved.T


def filter_kernel(
    got_ref, features_ref,
    part_ref, beyond_ref, own_ref, above_ref, below_ref,
    rows_ref, cols_ref, left_ref, map_ref, turned_ref,
):
    weights_of(got_ref, rows_ref, cols_ref)
    turn_rows(features_ref[...], turned_ref)
    map_ref[: 2 * MW] = jnp.zeros((2 * MW, C), BF16)
    map_ref[(2 + EXT) * MW :] = jnp.zeros((4 * MW, C), BF16)
    for start in range(0, EXT, ROWS):
        count = min(ROWS, EXT - start)
        part = rows_of(start, count, got_ref, rows_ref, cols_ref, left_ref)
        rounded = part.astype(BF16)
        map_ref[(2 + start) * MW : (2 + start + count) * MW] = rounded
        for h in range(start, start + count):
            one = slice((h - start) * MW, (h - start + 1) * MW)
            if h <= TR:
                own_ref[h * MW : (h + 1) * MW] = part[one]
            if h == 0:
                below_ref[...] = rounded[one]
                map_ref[(4 + EXT) * MW : (5 + EXT) * MW] = rounded[one]
            if h >= TR - 1:
                above_ref[(h - TR + 1) * MW : (h - TR + 2) * MW] = rounded[one]
    beyond_ref[...] = map_ref[(1 + TR) * MW : (3 + 2 * TR) * MW]
    for a in range(3):
        part_ref[a] = jnp.dot(
            turned_ref[...],
            map_ref[(3 - a) * MW : (3 - a + TR) * MW],
            preferred_element_type=F32,
        )


def beyond_kernel(
    core_ref, part_ref, beyond_ref, before_ref, after_ref, keep_ref, give_ref, turned_ref
):
    rows = jnp.concatenate([after_ref[...], before_ref[...], jnp.zeros((MW, C), BF16)], axis=0)
    turn_rows(rows, turned_ref)
    first = core_ref[0] == 0
    for a in range(3):
        part = part_ref[a] + jnp.dot(
            turned_ref[...],
            beyond_ref[(2 - a) * MW : (2 - a + TR) * MW],
            preferred_element_type=F32,
        )
        part = part.reshape(3, CHIPS, 2, CIN, C)
        for e in range(3):
            at = (a * 3 + e) * CIN
            keep_ref[:, at : at + CIN, :] = jnp.where(first, part[e, :, 0], part[e, :, 1])
            give_ref[:, at : at + CIN, :] = jnp.where(first, part[e, :, 1], part[e, :, 0]).astype(BF16)


def beyond_part(core, part, beyond, before, after):
    return pl.pallas_call(
        beyond_kernel,
        out_shape=(
            jax.ShapeDtypeStruct((CHIPS, NPART, C), F32),
            jax.ShapeDtypeStruct((CHIPS, NPART, C), BF16),
        ),
        in_specs=[pl.BlockSpec(memory_space=pltpu.SMEM)] + [vmem()] * 4,
        out_specs=(vmem(), vmem()),
        scratch_shapes=[pltpu.VMEM((3 * C, TR * MW), BF16)],
        compiler_params=pltpu.CompilerParams(vmem_limit_bytes=16 << 20),
        name="beyond",
        cost_estimate=cost(18 * TR * MW * C * C, 4 << 20),
    )(core, part, beyond, before, after)


def filter_part(got, features):
    return pl.pallas_call(
        filter_kernel,
        out_shape=(
            jax.ShapeDtypeStruct((3, 3 * C, C), F32),
            jax.ShapeDtypeStruct(((TR + 2) * MW, C), BF16),
            jax.ShapeDtypeStruct(((TR + 1) * MW, C), F32),
            jax.ShapeDtypeStruct((REACH * MW, C), BF16),
            jax.ShapeDtypeStruct((MW, C), BF16),
        ),
        in_specs=[vmem(), vmem()],
        out_specs=(vmem(),) * 5,
        scratch_shapes=[
            pltpu.VMEM((32, KDIM), F32),
            pltpu.VMEM((MW, KDIM), BF16),
            pltpu.VMEM((ROWS * MW, KDIM), BF16),
            pltpu.VMEM(((EXT + 6) * MW, C), BF16),
            pltpu.VMEM((3 * C, TR * MW), BF16),
        ],
        compiler_params=pltpu.CompilerParams(vmem_limit_bytes=30 << 20),
        name="filter",
        cost_estimate=cost(2 * EXT * MW * KDIM * C + 36 * TR * MW * C * C, 4 << 20),
    )(got, features)


def input_kernel(own_ref, above_ref, below_ref, weight_ref, out_ref, shifted_ref):
    whole = jnp.concatenate(
        [
            above_ref[:MW].astype(F32),
            own_ref[: (REACH - 1) * MW] + above_ref[MW:].astype(F32),
            own_ref[(REACH - 1) * MW : TR * MW],
            own_ref[TR * MW :] + below_ref[...].astype(F32),
        ],
        axis=0,
    )
    for e, moved in shifts(whole, 2, 0).items():
        shifted_ref[e] = moved
    total = jnp.zeros((TR * MW, C), F32)
    for a in range(3):
        for e in range(3):
            total = total + lax.dot_general(
                shifted_ref[e, (2 - a) * MW : (2 - a + TR) * MW],
                weight_ref[a * 3 + e],
                (((1,), (1,)), ((), ())),
                preferred_element_type=F32,
            )
    out_ref[...] = total.astype(BF16)


def input_part(own, above, below, weight):
    return pl.pallas_call(
        input_kernel,
        out_shape=jax.ShapeDtypeStruct((TR * MW, C), BF16),
        in_specs=[vmem()] * 4,
        out_specs=vmem(),
        scratch_shapes=[pltpu.VMEM((3, (TR + 2) * MW, C), BF16)],
        compiler_params=pltpu.CompilerParams(vmem_limit_bytes=16 << 20),
        name="input",
        cost_estimate=cost(18 * TR * MW * C * C, 4 << 20),
    )(own, above, below, weight)


def sum_kernel(scale, parts_ref, out_ref):
    total = parts_ref[0].astype(F32)
    for i in range(1, parts_ref.shape[0]):
        total = total + parts_ref[i].astype(F32)
    out_ref[...] = jnp.broadcast_to((total * scale).astype(out_ref.dtype), out_ref.shape)


def sum_parts(parts, shape, dtype, scale=1.0):
    return pl.pallas_call(
        functools.partial(sum_kernel, scale),
        out_shape=jax.ShapeDtypeStruct(shape, dtype),
        in_specs=[vmem()],
        out_specs=vmem(),
        compiler_params=pltpu.CompilerParams(vmem_limit_bytes=4 << 20),
        name="sum",
        cost_estimate=cost(parts.size, parts.size * 2),
    )(parts)


def pair_kernel(keep_ref, got_ref, out_ref):
    out_ref[...] = (keep_ref[...] + got_ref[...].astype(F32)).astype(BF16)


def sum_pair(keep, got):
    return pl.pallas_call(
        pair_kernel,
        out_shape=jax.ShapeDtypeStruct(keep.shape, BF16),
        in_specs=[vmem()] * 2,
        out_specs=vmem(),
        compiler_params=pltpu.CompilerParams(vmem_limit_bytes=4 << 20),
        name="pair",
        cost_estimate=cost(keep.size, keep.size * 8),
    )(keep, got)


def exchange(parts, axis):
    return lax.all_to_all(parts, axis, split_axis=0, concat_axis=0, tiled=True)


def body(features, weight, pool_grad, hard_index, boxes):
    grads = pool_grad[0].transpose(1, 2, 0, 3).reshape(CELLS, ROI_DEV, C)
    send = dispatch(hard_index, boxes[0].T, grads)
    up = [(t, t + 1) for t in range(TILES - 1)]
    down = [(b, a) for a, b in up]
    feature_rows = features[0].reshape(TR * MW, C)
    before = lax.ppermute(feature_rows[(TR - 1) * MW :], TILE_AXES, up)
    after = lax.ppermute(feature_rows[: REACH * MW], TILE_AXES, down)
    got = exchange(send, TILE_AXES)
    core = lax.axis_index("core").reshape(1)
    part, beyond, own, above, below = filter_part(got, feature_rows)
    keep, give = beyond_part(core, part, beyond, before, after)
    taken = lax.ppermute(give, "core", [(0, 1), (1, 0)])
    parts = exchange(sum_pair(keep, taken), "chip")
    below = lax.ppermute(below, TILE_AXES, down)
    parts, below = lax.optimization_barrier((parts, below))
    parts = exchange(sum_parts(parts, (4, NPART, C), BF16), "zl")
    above = lax.ppermute(above, TILE_AXES, up)
    x_grad = input_part(own, above, below, weight.reshape(9, C, C)).reshape(1, TR, MW, C)
    parts, x_grad = lax.optimization_barrier((parts, x_grad))
    parts = sum_parts(parts, (1, NPART, C), BF16)
    parts = lax.all_gather(parts, "zh", tiled=True, axis_index_groups=[[0, 1], [2, 3]])
    parts = sum_parts(parts, (1, NPART, C), BF16)
    parts = lax.all_gather(parts, "zh", tiled=True, axis_index_groups=[[0, 3], [1, 2]])
    total = sum_parts(parts, (NPART, C), F32, 1.0 / IMAGES)
    total = total.reshape(9, CIN, C).transpose(1, 0, 2).reshape(CIN, 3, 3, C)
    return x_grad, total


def solution(mesh):
    split = Mesh(mesh.devices.reshape(4, 4, CHIPS, 2), ("zh", "zl", "chip", "core"))
    images = ("zh", "zl")
    return jax.shard_map(
        body,
        mesh=split,
        in_specs=(
            P(images, TILE_AXES, None, None),
            P(),
            P(images, TILE_AXES, None, None, None),
            P(images, TILE_AXES),
            P(images, None, None),
        ),
        out_specs=(P(images, TILE_AXES, None, None), P(TILE_AXES, None, None, None)),
        check_vma=False,
    )
```

```python
import functools

import jax
import jax.numpy as jnp
from jax import lax
from jax.experimental import pallas as pl
from jax.experimental.pallas import tpu as pltpu
from jax.sharding import Mesh, PartitionSpec as P

C = 256
TR = 16
MW = 64
ROI_DEV = 16
CAP = 2
REACH = 14
BINS = 7
CELLS = BINS * BINS
PROPS = 20000
TILES = 32
CHIPS = TILES // 2
IMAGES = 16
EXT = TR + REACH - 1
ROWS = 3
SLOT = CELLS + 1
BLOCK = 104
SLOTS = TILES * CAP
KDIM = TILES * BLOCK
LANES = 128
WHOLE = PROPS // LANES * LANES
F32 = jnp.float32
BF16 = jnp.bfloat16
I32 = jnp.int32
CIN = C // TILES
TILE_AXES = ("chip", "core")
NPART = 9 * CIN


def vmem():
    return pl.BlockSpec(memory_space=pltpu.VMEM)


def cost(flops, moved):
    return pl.CostEstimate(flops=flops, bytes_accessed=moved, transcendentals=0)


def iota(shape, dim):
    return lax.broadcasted_iota(I32, shape, dim)


def dispatch_kernel(index_ref, boxes_ref, grad_ref, out_ref):
    lane16 = iota((4, ROI_DEV), 1)
    lanes = iota((4, LANES), 1)
    tail = jnp.concatenate(
        [boxes_ref[:, WHOLE:], jnp.zeros((4, LANES - (PROPS - WHOLE)), I32)], axis=1
    )
    chosen = jnp.zeros((4, ROI_DEV), I32)
    for r in range(ROI_DEV):
        index = index_ref[0, r]
        block = index // LANES
        at = jnp.minimum(block, WHOLE // LANES - 1) * LANES
        row = jnp.where(
            block == WHOLE // LANES, tail, boxes_ref[:, pl.ds(pl.multiple_of(at, LANES), LANES)]
        )
        found = jnp.sum(jnp.where(lanes == index - block * LANES, row, 0), axis=1, keepdims=True)
        chosen = jnp.where(lane16 == r, found, chosen)
    chosen = chosen.astype(F32)
    top = chosen[0:1]
    owner = jnp.floor(top * (1.0 / TR))
    local_top = top - owner * TR
    diag = iota((ROI_DEV, ROI_DEV), 0) == iota((ROI_DEV, ROI_DEV), 1)

    def column(row):
        wide = jnp.broadcast_to(row, (ROI_DEV, ROI_DEV))
        return jnp.sum(jnp.where(diag, wide, 0.0), axis=1, keepdims=True)

    before = iota((ROI_DEV, ROI_DEV), 0) < iota((ROI_DEV, ROI_DEV), 1)
    same = column(owner) == owner
    rank = jnp.sum(jnp.where(before & same, 1.0, 0.0), axis=0, keepdims=True)
    field = iota((ROI_DEV, C), 1)
    box_rows = jnp.zeros((ROI_DEV, C), F32)
    for f, row in enumerate((local_top, chosen[1:2], chosen[2:3], chosen[3:4])):
        box_rows = jnp.where(field == f, column(row), box_rows)
    depth = SLOT * ROI_DEV
    wide = jnp.concatenate([owner, rank, jnp.zeros((6, ROI_DEV), F32)], axis=0).astype(BF16)
    spreading = iota((ROI_DEV, depth), 1) % ROI_DEV == iota((ROI_DEV, depth), 0)
    spread = jnp.dot(wide, spreading.astype(F32).astype(BF16), preferred_element_type=F32)
    cell = (iota((1, depth), 1) // ROI_DEV).astype(F32)
    goal = (spread[0:1] * BLOCK + spread[1:2] * SLOT + cell).astype(I32)
    source = jnp.concatenate(
        [grad_ref[...].reshape(CELLS * ROI_DEV, C), box_rows.astype(BF16)], axis=0
    )
    step = KDIM // 8
    for m in range(8):
        place = iota((step, depth), 0) == goal - m * step
        out_ref[m * (TILES // 8) : (m + 1) * (TILES // 8)] = (
            jnp.dot(place.astype(F32).astype(BF16), source, preferred_element_type=F32)
            .astype(BF16)
            .reshape(TILES // 8, BLOCK, C)
        )


def dispatch(index, boxes_t, grads):
    return pl.pallas_call(
        dispatch_kernel,
        out_shape=jax.ShapeDtypeStruct((TILES, BLOCK, C), BF16),
        in_specs=[pl.BlockSpec(memory_space=pltpu.SMEM), vmem(), vmem()],
        out_specs=vmem(),
        compiler_params=pltpu.CompilerParams(vmem_limit_bytes=60 << 20),
        name="dispatch",
        cost_estimate=cost(2 * KDIM * SLOT * ROI_DEV * C, 3 << 20),
    )(index, boxes_t, grads)


def weights_of(got_ref, rows_ref, cols_ref):
    lane = iota((1, KDIM), 1)
    source = lane // BLOCK
    within = lane - source * BLOCK
    later = (within >= SLOT).astype(I32)
    within = within - later * SLOT
    inside = within < CELLS
    slot = jnp.where(inside, source + later * TILES, -1)
    box = jnp.concatenate(
        [got_ref[:, s * SLOT + CELLS, :LANES].astype(F32) for s in range(CAP)], axis=0
    )
    box = box.T[:8].astype(BF16)
    cover = (iota((SLOTS, KDIM), 0) == slot).astype(F32).astype(BF16)
    field = jnp.dot(box, cover, preferred_element_type=F32).astype(I32)
    row_bin = within // BINS
    col_bin = within - row_bin * BINS
    row = jnp.where(inside, field[0:1] + row_bin * field[2:3], -9)
    col = field[1:2] + col_bin * field[3:4]
    grid = iota((32, KDIM), 0)
    rows_ref[...] = jnp.where(grid == row, 0.75, jnp.where(grid == row + 1, 0.25, 0.0))
    grid = iota((MW, KDIM), 0)
    cols_ref[...] = jnp.where(grid == col, 0.25, jnp.where(grid == col + 1, 0.75, 0.0)).astype(BF16)


def rows_of(start, count, got_ref, rows_ref, cols_ref, left_ref):
    cols = cols_ref[...]
    for h in range(count):
        left_ref[h * MW : (h + 1) * MW] = cols * rows_ref[start + h : start + h + 1, :].astype(BF16)
    return jnp.dot(
        left_ref[: count * MW], got_ref[...].reshape(KDIM, C), preferred_element_type=F32
    )


def shifts(rows, before, after):
    count = rows.shape[0]
    column = iota((count, C), 0) % MW
    one_less = jnp.where(column == 0, 0.0, pltpu.roll(rows, 1, 0)).astype(BF16)
    one_more = jnp.where(column == MW - 1, 0.0, pltpu.roll(rows, count - 1, 0)).astype(BF16)
    return {before: one_less, 1: rows.astype(BF16), after: one_more}


def turn_rows(rows, out_ref):
    for e, moved in shifts(rows.astype(F32), 0, 2).items():
        out_ref[e * C : (e + 1) * C] = moved.T


def filter_kernel(
    got_ref, features_ref,
    part_ref, beyond_ref, own_ref, above_ref, below_ref,
    rows_ref, cols_ref, left_ref, map_ref, turned_ref,
):
    weights_of(got_ref, rows_ref, cols_ref)
    turn_rows(features_ref[...], turned_ref)
    map_ref[: 2 * MW] = jnp.zeros((2 * MW, C), BF16)
    map_ref[(2 + EXT) * MW :] = jnp.zeros((4 * MW, C), BF16)
    for start in range(0, EXT, ROWS):
        count = min(ROWS, EXT - start)
        part = rows_of(start, count, got_ref, rows_ref, cols_ref, left_ref)
        rounded = part.astype(BF16)
        map_ref[(2 + start) * MW : (2 + start + count) * MW] = rounded
        for h in range(start, start + count):
            one = slice((h - start) * MW, (h - start + 1) * MW)
            if h <= TR:
                own_ref[h * MW : (h + 1) * MW] = part[one]
            if h == 0:
                below_ref[...] = rounded[one]
                map_ref[(4 + EXT) * MW : (5 + EXT) * MW] = rounded[one]
            if h >= TR - 1:
                above_ref[(h - TR + 1) * MW : (h - TR + 2) * MW] = rounded[one]
    beyond_ref[...] = map_ref[(1 + TR) * MW : (3 + 2 * TR) * MW]
    for a in range(3):
        part_ref[a] = jnp.dot(
            turned_ref[...],
            map_ref[(3 - a) * MW : (3 - a + TR) * MW],
            preferred_element_type=F32,
        )


def beyond_kernel(
    core_ref, part_ref, beyond_ref, before_ref, after_ref, keep_ref, give_ref, turned_ref
):
    rows = jnp.concatenate([after_ref[...], before_ref[...], jnp.zeros((MW, C), BF16)], axis=0)
    turn_rows(rows, turned_ref)
    first = core_ref[0] == 0
    for a in range(3):
        part = part_ref[a] + jnp.dot(
            turned_ref[...],
            beyond_ref[(2 - a) * MW : (2 - a + TR) * MW],
            preferred_element_type=F32,
        )
        part = part.reshape(3, CHIPS, 2, CIN, C)
        for e in range(3):
            at = (a * 3 + e) * CIN
            keep_ref[:, at : at + CIN, :] = jnp.where(first, part[e, :, 0], part[e, :, 1])
            give_ref[:, at : at + CIN, :] = jnp.where(first, part[e, :, 1], part[e, :, 0]).astype(BF16)


def beyond_part(core, part, beyond, before, after):
    return pl.pallas_call(
        beyond_kernel,
        out_shape=(
            jax.ShapeDtypeStruct((CHIPS, NPART, C), F32),
            jax.ShapeDtypeStruct((CHIPS, NPART, C), BF16),
        ),
        in_specs=[pl.BlockSpec(memory_space=pltpu.SMEM)] + [vmem()] * 4,
        out_specs=(vmem(), vmem()),
        scratch_shapes=[pltpu.VMEM((3 * C, TR * MW), BF16)],
        compiler_params=pltpu.CompilerParams(vmem_limit_bytes=16 << 20),
        name="beyond",
        cost_estimate=cost(18 * TR * MW * C * C, 4 << 20),
    )(core, part, beyond, before, after)


def filter_part(got, features):
    return pl.pallas_call(
        filter_kernel,
        out_shape=(
            jax.ShapeDtypeStruct((3, 3 * C, C), F32),
            jax.ShapeDtypeStruct(((TR + 2) * MW, C), BF16),
            jax.ShapeDtypeStruct(((TR + 1) * MW, C), F32),
            jax.ShapeDtypeStruct((REACH * MW, C), BF16),
            jax.ShapeDtypeStruct((MW, C), BF16),
        ),
        in_specs=[vmem(), vmem()],
        out_specs=(vmem(),) * 5,
        scratch_shapes=[
            pltpu.VMEM((32, KDIM), F32),
            pltpu.VMEM((MW, KDIM), BF16),
            pltpu.VMEM((ROWS * MW, KDIM), BF16),
            pltpu.VMEM(((EXT + 6) * MW, C), BF16),
            pltpu.VMEM((3 * C, TR * MW), BF16),
        ],
        compiler_params=pltpu.CompilerParams(vmem_limit_bytes=30 << 20),
        name="filter",
        cost_estimate=cost(2 * EXT * MW * KDIM * C + 36 * TR * MW * C * C, 4 << 20),
    )(got, features)


def input_kernel(own_ref, above_ref, below_ref, weight_ref, out_ref, shifted_ref):
    whole = jnp.concatenate(
        [
            above_ref[:MW].astype(F32),
            own_ref[: (REACH - 1) * MW] + above_ref[MW:].astype(F32),
            own_ref[(REACH - 1) * MW : TR * MW],
            own_ref[TR * MW :] + below_ref[...].astype(F32),
        ],
        axis=0,
    )
    for e, moved in shifts(whole, 2, 0).items():
        shifted_ref[e] = moved
    total = jnp.zeros((TR * MW, C), F32)
    for a in range(3):
        for e in range(3):
            total = total + lax.dot_general(
                shifted_ref[e, (2 - a) * MW : (2 - a + TR) * MW],
                weight_ref[a * 3 + e],
                (((1,), (1,)), ((), ())),
                preferred_element_type=F32,
            )
    out_ref[...] = total.astype(BF16)


def input_part(own, above, below, weight):
    return pl.pallas_call(
        input_kernel,
        out_shape=jax.ShapeDtypeStruct((TR * MW, C), BF16),
        in_specs=[vmem()] * 4,
        out_specs=vmem(),
        scratch_shapes=[pltpu.VMEM((3, (TR + 2) * MW, C), BF16)],
        compiler_params=pltpu.CompilerParams(vmem_limit_bytes=16 << 20),
        name="input",
        cost_estimate=cost(18 * TR * MW * C * C, 4 << 20),
    )(own, above, below, weight)


def sum_kernel(scale, parts_ref, out_ref):
    total = parts_ref[0].astype(F32)
    for i in range(1, parts_ref.shape[0]):
        total = total + parts_ref[i].astype(F32)
    out_ref[...] = jnp.broadcast_to((total * scale).astype(out_ref.dtype), out_ref.shape)


def sum_parts(parts, shape, dtype, scale=1.0):
    return pl.pallas_call(
        functools.partial(sum_kernel, scale),
        out_shape=jax.ShapeDtypeStruct(shape, dtype),
        in_specs=[vmem()],
        out_specs=vmem(),
        compiler_params=pltpu.CompilerParams(vmem_limit_bytes=4 << 20),
        name="sum",
        cost_estimate=cost(parts.size, parts.size * 2),
    )(parts)


def pair_kernel(keep_ref, got_ref, out_ref):
    out_ref[...] = (keep_ref[...] + got_ref[...].astype(F32)).astype(BF16)


def sum_pair(keep, got):
    return pl.pallas_call(
        pair_kernel,
        out_shape=jax.ShapeDtypeStruct(keep.shape, BF16),
        in_specs=[vmem()] * 2,
        out_specs=vmem(),
        compiler_params=pltpu.CompilerParams(vmem_limit_bytes=4 << 20),
        name="pair",
        cost_estimate=cost(keep.size, keep.size * 8),
    )(keep, got)


def exchange(parts, axis):
    return lax.all_to_all(parts, axis, split_axis=0, concat_axis=0, tiled=True)


def body(features, weight, pool_grad, hard_index, boxes):
    grads = pool_grad[0].transpose(1, 2, 0, 3).reshape(CELLS, ROI_DEV, C)
    send = dispatch(hard_index, boxes[0].T, grads)
    up = [(t, t + 1) for t in range(TILES - 1)]
    down = [(b, a) for a, b in up]
    feature_rows = features[0].reshape(TR * MW, C)
    before = lax.ppermute(feature_rows[(TR - 1) * MW :], TILE_AXES, up)
    after = lax.ppermute(feature_rows[: REACH * MW], TILE_AXES, down)
    got = exchange(send, TILE_AXES)
    core = lax.axis_index("core").reshape(1)
    part, beyond, own, above, below = filter_part(got, feature_rows)
    keep, give = beyond_part(core, part, beyond, before, after)
    taken = lax.ppermute(give, "core", [(0, 1), (1, 0)])
    parts = exchange(sum_pair(keep, taken), "chip")
    below = lax.ppermute(below, TILE_AXES, down)
    parts, below = lax.optimization_barrier((parts, below))
    parts = exchange(sum_parts(parts, (4, NPART, C), BF16), "zl")
    above = lax.ppermute(above, TILE_AXES, up)
    x_grad = input_part(own, above, below, weight.reshape(9, C, C)).reshape(1, TR, MW, C)
    parts, x_grad = lax.optimization_barrier((parts, x_grad))
    parts = sum_parts(parts, (1, NPART, C), BF16)
    parts = lax.all_gather(parts, "zh", tiled=True, axis_index_groups=[[0, 1], [2, 3]])
    parts = sum_parts(parts, (1, NPART, C), BF16)
    parts = lax.all_gather(parts, "zh", tiled=True, axis_index_groups=[[0, 3], [1, 2]])
    total = sum_parts(parts, (NPART, C), F32, 1.0 / IMAGES)
    total = total.reshape(9, CIN, C).transpose(1, 0, 2).reshape(CIN, 3, 3, C)
    return x_grad, total


def solution(mesh):
    split = Mesh(mesh.devices.reshape(4, 4, CHIPS, 2), ("zh", "zl", "chip", "core"))
    images = ("zh", "zl")
    return jax.shard_map(
        body,
        mesh=split,
        in_specs=(
            P(images, TILE_AXES, None, None),
            P(),
            P(images, TILE_AXES, None, None, None),
            P(images, TILE_AXES),
            P(images, None, None),
        ),
        out_specs=(P(images, TILE_AXES, None, None), P(TILE_AXES, None, None, None)),
        check_vma=False,
    )
```

```python
import functools

import jax
import jax.numpy as jnp
from jax import lax
from jax.experimental import pallas as pl
from jax.experimental.pallas import tpu as pltpu
from jax.sharding import Mesh, PartitionSpec as P

C = 256
TR = 16
MW = 64
ROI_DEV = 16
CAP = 2
REACH = 14
BINS = 7
CELLS = BINS * BINS
PROPS = 20000
TILES = 32
CHIPS = TILES // 2
IMAGES = 16
EXT = TR + REACH - 1
ROWS = 3
SLOT = CELLS + 1
BLOCK = 104
SLOTS = TILES * CAP
KDIM = TILES * BLOCK
LANES = 128
WHOLE = PROPS // LANES * LANES
F32 = jnp.float32
BF16 = jnp.bfloat16
I32 = jnp.int32
CIN = C // TILES
TILE_AXES = ("chip", "core")
NPART = 9 * CIN


def vmem():
    return pl.BlockSpec(memory_space=pltpu.VMEM)


def hbm():
    return pl.BlockSpec(memory_space=pltpu.HBM)


def cost(flops, moved):
    return pl.CostEstimate(flops=flops, bytes_accessed=moved, transcendentals=0)


def iota(shape, dim):
    return lax.broadcasted_iota(I32, shape, dim)


def dispatch_kernel(
    index_hbm, boxes_hbm, grad_hbm, out_hbm, index_ref, boxes_ref, source_ref, sent_ref, sems
):
    copies = [
        pltpu.make_async_copy(index_hbm, index_ref, sems.at[0]),
        pltpu.make_async_copy(boxes_hbm, boxes_ref, sems.at[1]),
        pltpu.make_async_copy(grad_hbm, source_ref.at[:CELLS], sems.at[2]),
    ]
    for copy in copies:
        copy.start()
    copies[0].wait()
    copies[1].wait()
    lane16 = iota((4, ROI_DEV), 1)
    lanes = iota((4, LANES), 1)
    tail = jnp.concatenate(
        [boxes_ref[:, WHOLE:], jnp.zeros((4, LANES - (PROPS - WHOLE)), I32)], axis=1
    )
    chosen = jnp.zeros((4, ROI_DEV), I32)
    for r in range(ROI_DEV):
        index = index_ref[0, r]
        block = index // LANES
        at = jnp.minimum(block, WHOLE // LANES - 1) * LANES
        row = jnp.where(
            block == WHOLE // LANES, tail, boxes_ref[:, pl.ds(pl.multiple_of(at, LANES), LANES)]
        )
        found = jnp.sum(jnp.where(lanes == index - block * LANES, row, 0), axis=1, keepdims=True)
        chosen = jnp.where(lane16 == r, found, chosen)
    chosen = chosen.astype(F32)
    top = chosen[0:1]
    owner = jnp.floor(top * (1.0 / TR))
    local_top = top - owner * TR
    diag = iota((ROI_DEV, ROI_DEV), 0) == iota((ROI_DEV, ROI_DEV), 1)

    def column(row):
        wide = jnp.broadcast_to(row, (ROI_DEV, ROI_DEV))
        return jnp.sum(jnp.where(diag, wide, 0.0), axis=1, keepdims=True)

    before = iota((ROI_DEV, ROI_DEV), 0) < iota((ROI_DEV, ROI_DEV), 1)
    same = column(owner) == owner
    rank = jnp.sum(jnp.where(before & same, 1.0, 0.0), axis=0, keepdims=True)
    field = iota((ROI_DEV, C), 1)
    box_rows = jnp.zeros((ROI_DEV, C), F32)
    for f, row in enumerate((local_top, chosen[1:2], chosen[2:3], chosen[3:4])):
        box_rows = jnp.where(field == f, column(row), box_rows)
    source_ref[CELLS] = box_rows.astype(BF16)
    depth = SLOT * ROI_DEV
    wide = jnp.concatenate([owner, rank, jnp.zeros((6, ROI_DEV), F32)], axis=0).astype(BF16)
    spreading = iota((ROI_DEV, depth), 1) % ROI_DEV == iota((ROI_DEV, depth), 0)
    spread = jnp.dot(wide, spreading.astype(F32).astype(BF16), preferred_element_type=F32)
    cell = (iota((1, depth), 1) // ROI_DEV).astype(F32)
    goal = (spread[0:1] * BLOCK + spread[1:2] * SLOT + cell).astype(I32)
    copies[2].wait()
    source = source_ref[...].reshape(depth, C)
    step = KDIM // 8
    sent = []
    for m in range(8):
        part = pl.ds(m * (TILES // 8), TILES // 8)
        place = iota((step, depth), 0) == goal - m * step
        sent_ref[part] = (
            jnp.dot(place.astype(F32).astype(BF16), source, preferred_element_type=F32)
            .astype(BF16)
            .reshape(TILES // 8, BLOCK, C)
        )
        sent.append(pltpu.make_async_copy(sent_ref.at[part], out_hbm.at[part], sems.at[3 + m]))
        sent[-1].start()
    for copy in sent:
        copy.wait()


def dispatch(index, boxes_t, grads):
    return pl.pallas_call(
        dispatch_kernel,
        out_shape=jax.ShapeDtypeStruct((TILES, BLOCK, C), BF16),
        in_specs=[pl.BlockSpec(memory_space=pl.ANY)] * 3,
        out_specs=pl.BlockSpec(memory_space=pl.ANY),
        scratch_shapes=[
            pltpu.SMEM((1, ROI_DEV), I32),
            pltpu.VMEM((4, PROPS), I32),
            pltpu.VMEM((SLOT, ROI_DEV, C), BF16),
            pltpu.VMEM((TILES, BLOCK, C), BF16),
            pltpu.SemaphoreType.DMA((11,)),
        ],
        compiler_params=pltpu.CompilerParams(vmem_limit_bytes=60 << 20),
        name="dispatch",
        cost_estimate=cost(2 * KDIM * SLOT * ROI_DEV * C, 3 << 20),
    )(*(pltpu.with_memory_space_constraint(x, pltpu.HBM) for x in (index, boxes_t, grads)))


def weights_of(got_ref, rows_ref, cols_ref):
    lane = iota((1, KDIM), 1)
    source = lane // BLOCK
    within = lane - source * BLOCK
    later = (within >= SLOT).astype(I32)
    within = within - later * SLOT
    inside = within < CELLS
    slot = jnp.where(inside, source + later * TILES, -1)
    box = jnp.concatenate(
        [got_ref[:, s * SLOT + CELLS, :LANES].astype(F32) for s in range(CAP)], axis=0
    )
    box = box.T[:8].astype(BF16)
    cover = (iota((SLOTS, KDIM), 0) == slot).astype(F32).astype(BF16)
    field = jnp.dot(box, cover, preferred_element_type=F32).astype(I32)
    row_bin = within // BINS
    col_bin = within - row_bin * BINS
    row = jnp.where(inside, field[0:1] + row_bin * field[2:3], -9)
    col = field[1:2] + col_bin * field[3:4]
    grid = iota((32, KDIM), 0)
    rows_ref[...] = jnp.where(grid == row, 0.75, jnp.where(grid == row + 1, 0.25, 0.0))
    grid = iota((MW, KDIM), 0)
    cols_ref[...] = jnp.where(grid == col, 0.25, jnp.where(grid == col + 1, 0.75, 0.0)).astype(BF16)


def rows_of(start, count, got_ref, rows_ref, cols_ref, left_ref):
    cols = cols_ref[...]
    for h in range(count):
        left_ref[h * MW : (h + 1) * MW] = cols * rows_ref[start + h : start + h + 1, :].astype(BF16)
    return jnp.dot(
        left_ref[: count * MW], got_ref[...].reshape(KDIM, C), preferred_element_type=F32
    )


def shifts(rows, before, after):
    count = rows.shape[0]
    column = iota((count, C), 0) % MW
    one_less = jnp.where(column == 0, 0.0, pltpu.roll(rows, 1, 0)).astype(BF16)
    one_more = jnp.where(column == MW - 1, 0.0, pltpu.roll(rows, count - 1, 0)).astype(BF16)
    return {before: one_less, 1: rows.astype(BF16), after: one_more}


def turn_rows(rows, out_ref):
    for e, moved in shifts(rows.astype(F32), 0, 2).items():
        out_ref[e * C : (e + 1) * C] = moved.T


def filter_kernel(
    got_ref, features_ref,
    part_ref, beyond_ref, own_ref, above_ref, below_ref,
    rows_ref, cols_ref, left_ref, map_ref, turned_ref,
):
    weights_of(got_ref, rows_ref, cols_ref)
    turn_rows(features_ref[...], turned_ref)
    map_ref[: 2 * MW] = jnp.zeros((2 * MW, C), BF16)
    map_ref[(2 + EXT) * MW :] = jnp.zeros((4 * MW, C), BF16)
    for start in range(0, EXT, ROWS):
        count = min(ROWS, EXT - start)
        part = rows_of(start, count, got_ref, rows_ref, cols_ref, left_ref)
        rounded = part.astype(BF16)
        map_ref[(2 + start) * MW : (2 + start + count) * MW] = rounded
        for h in range(start, start + count):
            one = slice((h - start) * MW, (h - start + 1) * MW)
            if h <= TR:
                own_ref[h * MW : (h + 1) * MW] = part[one]
            if h == 0:
                below_ref[...] = rounded[one]
                map_ref[(4 + EXT) * MW : (5 + EXT) * MW] = rounded[one]
            if h >= TR - 1:
                above_ref[(h - TR + 1) * MW : (h - TR + 2) * MW] = rounded[one]
    beyond_ref[...] = map_ref[(1 + TR) * MW : (3 + 2 * TR) * MW]
    for a in range(3):
        part_ref[a] = jnp.dot(
            turned_ref[...],
            map_ref[(3 - a) * MW : (3 - a + TR) * MW],
            preferred_element_type=F32,
        )


def beyond_kernel(
    core_ref, part_ref, beyond_ref, before_ref, after_ref, keep_ref, give_ref, turned_ref
):
    rows = jnp.concatenate([after_ref[...], before_ref[...], jnp.zeros((MW, C), BF16)], axis=0)
    turn_rows(rows, turned_ref)
    first = core_ref[0] == 0
    for a in range(3):
        part = part_ref[a] + jnp.dot(
            turned_ref[...],
            beyond_ref[(2 - a) * MW : (2 - a + TR) * MW],
            preferred_element_type=F32,
        )
        part = part.reshape(3, CHIPS, 2, CIN, C)
        for e in range(3):
            at = (a * 3 + e) * CIN
            keep_ref[:, at : at + CIN, :] = jnp.where(first, part[e, :, 0], part[e, :, 1])
            give_ref[:, at : at + CIN, :] = jnp.where(first, part[e, :, 1], part[e, :, 0]).astype(BF16)


def beyond_part(core, part, beyond, before, after):
    return pl.pallas_call(
        beyond_kernel,
        out_shape=(
            jax.ShapeDtypeStruct((CHIPS, NPART, C), F32),
            jax.ShapeDtypeStruct((CHIPS, NPART, C), BF16),
        ),
        in_specs=[pl.BlockSpec(memory_space=pltpu.SMEM)] + [vmem()] * 4,
        out_specs=(vmem(), vmem()),
        scratch_shapes=[pltpu.VMEM((3 * C, TR * MW), BF16)],
        compiler_params=pltpu.CompilerParams(vmem_limit_bytes=16 << 20),
        name="beyond",
        cost_estimate=cost(18 * TR * MW * C * C, 4 << 20),
    )(core, part, beyond, before, after)


def filter_part(got, features):
    return pl.pallas_call(
        filter_kernel,
        out_shape=(
            jax.ShapeDtypeStruct((3, 3 * C, C), F32),
            jax.ShapeDtypeStruct(((TR + 2) * MW, C), BF16),
            jax.ShapeDtypeStruct(((TR + 1) * MW, C), F32),
            jax.ShapeDtypeStruct((REACH * MW, C), BF16),
            jax.ShapeDtypeStruct((MW, C), BF16),
        ),
        in_specs=[vmem(), vmem()],
        out_specs=(vmem(),) * 5,
        scratch_shapes=[
            pltpu.VMEM((32, KDIM), F32),
            pltpu.VMEM((MW, KDIM), BF16),
            pltpu.VMEM((ROWS * MW, KDIM), BF16),
            pltpu.VMEM(((EXT + 6) * MW, C), BF16),
            pltpu.VMEM((3 * C, TR * MW), BF16),
        ],
        compiler_params=pltpu.CompilerParams(vmem_limit_bytes=30 << 20),
        name="filter",
        cost_estimate=cost(2 * EXT * MW * KDIM * C + 36 * TR * MW * C * C, 4 << 20),
    )(got, features)


def input_kernel(own_ref, above_ref, below_ref, weight_ref, out_ref, shifted_ref):
    whole = jnp.concatenate(
        [
            above_ref[:MW].astype(F32),
            own_ref[: (REACH - 1) * MW] + above_ref[MW:].astype(F32),
            own_ref[(REACH - 1) * MW : TR * MW],
            own_ref[TR * MW :] + below_ref[...].astype(F32),
        ],
        axis=0,
    )
    for e, moved in shifts(whole, 2, 0).items():
        shifted_ref[e] = moved
    total = jnp.zeros((TR * MW, C), F32)
    for a in range(3):
        for e in range(3):
            total = total + lax.dot_general(
                shifted_ref[e, (2 - a) * MW : (2 - a + TR) * MW],
                weight_ref[a * 3 + e],
                (((1,), (1,)), ((), ())),
                preferred_element_type=F32,
            )
    out_ref[...] = total.astype(BF16)


def input_part(own, above, below, weight):
    return pl.pallas_call(
        input_kernel,
        out_shape=jax.ShapeDtypeStruct((TR * MW, C), BF16),
        in_specs=[vmem()] * 4,
        out_specs=vmem(),
        scratch_shapes=[pltpu.VMEM((3, (TR + 2) * MW, C), BF16)],
        compiler_params=pltpu.CompilerParams(vmem_limit_bytes=16 << 20),
        name="input",
        cost_estimate=cost(18 * TR * MW * C * C, 4 << 20),
    )(own, above, below, weight)


def sum_kernel(scale, parts_ref, out_ref):
    total = parts_ref[0].astype(F32)
    for i in range(1, parts_ref.shape[0]):
        total = total + parts_ref[i].astype(F32)
    out_ref[...] = jnp.broadcast_to((total * scale).astype(out_ref.dtype), out_ref.shape)


def sum_parts(parts, shape, dtype, scale=1.0):
    return pl.pallas_call(
        functools.partial(sum_kernel, scale),
        out_shape=jax.ShapeDtypeStruct(shape, dtype),
        in_specs=[vmem()],
        out_specs=vmem(),
        compiler_params=pltpu.CompilerParams(vmem_limit_bytes=4 << 20),
        name="sum",
        cost_estimate=cost(parts.size, parts.size * 2),
    )(parts)


def pair_kernel(keep_ref, got_ref, out_ref):
    out_ref[...] = (keep_ref[...] + got_ref[...].astype(F32)).astype(BF16)


def sum_pair(keep, got):
    return pl.pallas_call(
        pair_kernel,
        out_shape=jax.ShapeDtypeStruct(keep.shape, BF16),
        in_specs=[vmem()] * 2,
        out_specs=vmem(),
        compiler_params=pltpu.CompilerParams(vmem_limit_bytes=4 << 20),
        name="pair",
        cost_estimate=cost(keep.size, keep.size * 8),
    )(keep, got)


def exchange(parts, axis):
    return lax.all_to_all(parts, axis, split_axis=0, concat_axis=0, tiled=True)


def body(features, weight, pool_grad, hard_index, boxes):
    grads = pool_grad[0].transpose(1, 2, 0, 3).reshape(CELLS, ROI_DEV, C)
    send = dispatch(hard_index, boxes[0].T, grads)
    up = [(t, t + 1) for t in range(TILES - 1)]
    down = [(b, a) for a, b in up]
    feature_rows = features[0].reshape(TR * MW, C)
    before = lax.ppermute(feature_rows[(TR - 1) * MW :], TILE_AXES, up)
    after = lax.ppermute(feature_rows[: REACH * MW], TILE_AXES, down)
    got = exchange(send, TILE_AXES)
    core = lax.axis_index("core").reshape(1)
    part, beyond, own, above, below = filter_part(got, feature_rows)
    keep, give = beyond_part(core, part, beyond, before, after)
    taken = lax.ppermute(give, "core", [(0, 1), (1, 0)])
    parts = exchange(sum_pair(keep, taken), "chip")
    below = lax.ppermute(below, TILE_AXES, down)
    parts, below = lax.optimization_barrier((parts, below))
    parts = exchange(sum_parts(parts, (4, NPART, C), BF16), "zl")
    above = lax.ppermute(above, TILE_AXES, up)
    x_grad = input_part(own, above, below, weight.reshape(9, C, C)).reshape(1, TR, MW, C)
    parts, x_grad = lax.optimization_barrier((parts, x_grad))
    parts = sum_parts(parts, (1, NPART, C), BF16)
    parts = lax.all_gather(parts, "zh", tiled=True, axis_index_groups=[[0, 1], [2, 3]])
    parts = sum_parts(parts, (1, NPART, C), BF16)
    parts = lax.all_gather(parts, "zh", tiled=True, axis_index_groups=[[0, 3], [1, 2]])
    total = sum_parts(parts, (NPART, C), F32, 1.0 / IMAGES)
    total = total.reshape(9, CIN, C).transpose(1, 0, 2).reshape(CIN, 3, 3, C)
    return x_grad, total


def solution(mesh):
    split = Mesh(mesh.devices.reshape(4, 4, CHIPS, 2), ("zh", "zl", "chip", "core"))
    images = ("zh", "zl")
    return jax.shard_map(
        body,
        mesh=split,
        in_specs=(
            P(images, TILE_AXES, None, None),
            P(),
            P(images, TILE_AXES, None, None, None),
            P(images, TILE_AXES),
            P(images, None, None),
        ),
        out_specs=(P(images, TILE_AXES, None, None), P(TILE_AXES, None, None, None)),
        check_vma=False,
    )
```
